256 devices in a mesh: ctx: 32 (over y_lo, z, core), ch: 8 (over x, y_hi).
Axes of the slice: x: 4, y: 4 (y_hi: 2, y_lo: 2; y = y_hi * 2 + y_lo), z: 8, core: 2. Of those that a mesh axis runs over, the one named last changes fastest.
Arguments:
- outer_gate: bfloat16 [8192, 4096], P('ctx', 'ch'), may hold values from -6 to 6
- inner_gate: bfloat16 [8192, 4096], P('ctx', 'ch'), may hold values from -6 to 6
- values: bfloat16 [8192, 4096], P('ctx', 'ch'), may hold values from -6 to 6
- residues: float32 [16, 4096], P(None, 'ch'), may hold values from -0.18 to 0.18
- decays: float32 [16, 4096], P(None, 'ch'), may hold values from 1.2207031e-05 to 0.05
- out_weight: bfloat16 [4096, 8192], P('ch', 'ctx'), may hold values from -0.1875 to 0.1875
Outputs:
- projected: bfloat16 [8192, 8192], P('ctx', 'ch')
The draws below stay inside these ranges and needn't reach their ends.
All inputs are finite; a program needn't handle non-finite values.
Results may differ from the reference program's by a relative error of at most 0.015.
Values may be sent and summed in bfloat16 or wider, within the bound.
No kernel may reach another device: no remote copies, remote signals or barrier semaphores. Data moves between devices by JAX's collectives and lax.ppermute only.
A program may use at most 64 MiB of HBM per device.

```python
import math
import jax
import jax.numpy as jnp
from jax import lax

D = 8192
SLAB = 4096
ORDER = 16
SEQ = 8192
FILT = 8192


def with_spikes(drawn, key, source, target, shards_of, factor):
    def block_of(dim):
        return (jnp.arange(drawn.shape[dim]) // (drawn.shape[dim] // shards_of)).reshape((-1,) + (1,) * (drawn.ndim - 1 - dim))

    one_side = jax.random.permutation(key, shards_of)[block_of(target)]
    second = (block_of(target) + shards_of // 2) % shards_of
    return jnp.where((block_of(source) == one_side) | (block_of(source) == second), factor * drawn, drawn)


def block_scale(stream_key, extent, shards, low, largest):
    gain, own = 1.0, jax.random.fold_in(stream_key, 6)
    for dim, blocks in shards:
        heights = jnp.exp(jax.random.uniform(jax.random.fold_in(own, dim), (blocks,), jnp.float32, low / len(shards), largest / len(shards)))
        gain = gain * jnp.repeat(heights, extent[dim] // blocks).reshape([-1 if axis == dim else 1 for axis in range(len(extent))])
    return gain


def bell_draw(stream_key, extent, deviation, most, split=(), kind=jnp.bfloat16):
    loudness = block_scale(stream_key, extent, split, -0.22, 0.18) if split else 1.0
    values = jax.random.normal(stream_key, extent, jnp.float32) * deviation * loudness
    return jnp.minimum(jnp.maximum(values, -most), most).astype(kind)


def bell_draw_with(own_key, extent, scale, reach, split, heavy, kind=jnp.bfloat16):
    array = scale * jax.random.normal(own_key, extent, jnp.float32)
    if split:
        array = array * block_scale(own_key, extent, split, -0.22, 0.18)
    return jnp.clip(with_spikes(array, jax.random.fold_in(own_key, 3), *heavy), -reach, reach).astype(kind)


def setup_inputs(seed: int = 0) -> dict:
    keys = jax.random.split(jax.random.key(seed), 7)
    return {
        "outer_gate": bell_draw(keys[0], (SEQ, SLAB), 1.0, 6.0, ((0, 32), (1, 8))),
        "inner_gate": bell_draw(keys[1], (SEQ, SLAB), 1.0, 6.0, ((0, 32), (1, 8))),
        "values": bell_draw(keys[2], (SEQ, SLAB), 1.0, 6.0, ((0, 32), (1, 8))),
        "residues": bell_draw(keys[3], (ORDER, SLAB), 0.03, 0.18, ((1, 8),), jnp.float32),
        "decays": jnp.clip(jnp.exp(math.log(0.05) - 8.317766 * jax.random.uniform(keys[4], (ORDER, SLAB), jnp.float32) ** block_scale(keys[4], (ORDER, SLAB), ((1, 8),), -0.2, 0.2)), 1.220703143189894e-05, 0.05),
        "out_weight": bell_draw_with(keys[5], (SLAB, D), SLAB ** -0.5, 0.1875, ((0, 8), (1, 32)), (0, 1, 32, 2.75)),
    }


def reference(outer_gate, inner_gate, values, residues, decays, out_weight):
    positions = values.shape[0]
    signal = (inner_gate.astype(jnp.float32) * values.astype(jnp.float32)).astype(jnp.bfloat16)
    lag_values = jnp.arange(FILT).astype(jnp.float32)

    def add_mode(total, mode):
        weight_row, decay_row = mode
        return total + weight_row[None, :] * jnp.exp(-decay_row[None, :] * lag_values[:, None]), None

    start_total = jnp.zeros((FILT, residues.shape[1]), residues.dtype)
    response, unused = lax.scan(add_mode, start_total, (residues, decays))
    padded_length = 2 * positions
    spectrum = jnp.fft.rfft(signal.astype(jnp.float32), n=padded_length, axis=0) * jnp.fft.rfft(response, n=padded_length, axis=0)
    convolved = jnp.fft.irfft(spectrum, n=padded_length, axis=0)[:positions]
    gated = (outer_gate.astype(jnp.float32) * convolved).astype(jnp.bfloat16)
    summed = jnp.dot(gated.astype(jnp.float32), out_weight.astype(jnp.float32), preferred_element_type=jnp.float32)
    return summed.astype(jnp.bfloat16)
```

```python
import jax
import jax.numpy as jnp
from jax import lax
from jax.experimental import pallas as pl
from jax.experimental.pallas import tpu as pltpu
from jax.sharding import Mesh
from jax.sharding import PartitionSpec as P

ROWS, CHANS, MODES = 256, 512, 16
SUB = 16
BLOCKS = ROWS // SUB
LANES = 128
TILES = CHANS // LANES
HALF = CHANS // 2
F32, BF16 = jnp.float32, jnp.bfloat16
VMEM_LIMIT = 48 * 1024 * 1024


def whole(n):
    return [pl.BlockSpec(memory_space=pltpu.VMEM)] * n


def call(body, outs, scratch, flops, moved, *args):
    return pl.pallas_call(
        body,
        out_shape=outs,
        in_specs=whole(len(args)),
        out_specs=whole(len(outs)) if isinstance(outs, (list, tuple)) else whole(1)[0],
        scratch_shapes=scratch,
        compiler_params=pltpu.CompilerParams(vmem_limit_bytes=VMEM_LIMIT),
        cost_estimate=pl.CostEstimate(flops=flops, bytes_accessed=moved, transcendentals=0),
    )(*args)


def signal_into(inner, values, sig):
    for lt in range(TILES):
        cols = slice(lt * LANES, (lt + 1) * LANES)
        product = inner[:, cols].astype(F32) * values[:, cols].astype(F32)
        sig[lt] = product.astype(BF16).astype(F32)


def sums_body(inner, values, decays, sums, keep, send, sig):
    signal_into(inner, values, sig)
    for lt in range(TILES):
        cols = slice(lt * LANES, (lt + 1) * LANES)
        fade = jnp.exp(-decays[:, cols])
        for group in range(0, MODES, 8):
            step = [jnp.broadcast_to(fade[r : r + 1], (BLOCKS, LANES)) for r in range(group, group + 8)]
            total = [sig[lt, pl.ds(0, BLOCKS, stride=SUB), :]] * 8
            for b in range(1, SUB):
                row = sig[lt, pl.ds(b, BLOCKS, stride=SUB), :]
                total = [t * e + row for t, e in zip(total, step)]
            for i in range(8):
                sums[lt, pl.ds(group + i, BLOCKS, stride=MODES), :] = total[i]
    core = lax.axis_index("core")
    for lt in range(TILES):
        cols = slice(lt * LANES, (lt + 1) * LANES)
        fade = jnp.exp(-decays[:, cols] * SUB)
        state = sums[lt, 0:MODES, :]
        for a in range(1, BLOCKS):
            state = state * fade + sums[lt, a * MODES : (a + 1) * MODES, :]
        place = slice((lt % 2) * LANES, (lt % 2 + 1) * LANES)

        @pl.when(core == lt // 2)
        def _():
            keep[:, place] = state

        @pl.when(core != lt // 2)
        def _():
            send[:, place] = state


def taps_body(inner, values, residues, decays, local, sig):
    signal_into(inner, values, sig)
    for lt in range(TILES):
        cols = slice(lt * LANES, (lt + 1) * LANES)
        fade = jnp.exp(-decays[:, cols])
        weight = residues[:, cols]
        taps = []
        for lag in range(SUB):
            taps.append(jnp.broadcast_to(jnp.sum(weight, axis=0, keepdims=True), (BLOCKS, LANES)))
            weight = weight * fade
        rows = [sig[lt, pl.ds(b, BLOCKS, stride=SUB), :] for b in range(SUB)]
        for b in range(SUB):
            total = taps[0] * rows[b]
            for lag in range(1, b + 1):
                total = total + taps[lag] * rows[b - lag]
            local[lt, pl.ds(b, BLOCKS, stride=SUB), :] = total


def gate_body(outer, sums, local, near, far, residues, decays, gated, states, out):
    core = lax.axis_index("core")
    for lt in range(TILES):
        cols = slice(lt * LANES, (lt + 1) * LANES)
        place = slice((lt % 2) * LANES, (lt % 2 + 1) * LANES)
        fade = jnp.exp(-decays[:, cols] * SUB)
        weight = residues[:, cols]
        state = jnp.where(core == lt // 2, near[:, place], far[:, place])
        for a in range(BLOCKS):
            states[lt, a * MODES : (a + 1) * MODES, :] = state * weight
            if a + 1 < BLOCKS:
                state = state * fade + sums[lt, a * MODES : (a + 1) * MODES, :]
    for lt in range(TILES):
        cols = slice(lt * LANES, (lt + 1) * LANES)
        fade = jnp.exp(-decays[:, cols])
        step = [jnp.broadcast_to(fade[r : r + 1], (BLOCKS, LANES)) for r in range(MODES)]
        part = [states[lt, pl.ds(r, BLOCKS, stride=MODES), :] for r in range(MODES)]
        for b in range(SUB):
            part = [t * e for t, e in zip(part, step)]
            total = part
            while len(total) > 1:
                total = [total[i] + total[i + 1] for i in range(0, len(total), 2)]
            out[lt, pl.ds(b, BLOCKS, stride=SUB), :] = total[0] + local[lt, pl.ds(b, BLOCKS, stride=SUB), :]
    for lt in range(TILES):
        cols = slice(lt * LANES, (lt + 1) * LANES)
        result = (outer[:, cols].astype(F32) * out[lt]).astype(BF16)
        for copy in range(gated.shape[0]):
            gated[copy, :, cols] = result


def project_body(places, *refs):
    own, other = refs[0], refs[1]
    blocks = refs[2 : 2 + len(places)]
    mine, theirs, acc = refs[2 + len(places) :]
    z, y = lax.axis_index("z"), lax.axis_index("ylo")
    acc[...] = jnp.zeros_like(acc)
    for block, (turn, shift) in zip(blocks, places):
        at = lax.rem(z + shift, 8)
        rank = lax.rem(y + turn, 2) * 4 + at // 2
        odd = lax.rem(at, 2)
        weight = block[...]
        acc[0, odd] += jnp.dot(own[rank], weight, preferred_element_type=F32)
        acc[1, odd] += jnp.dot(other[rank], weight, preferred_element_type=F32)
    mine[...] = acc[0].astype(BF16)
    theirs[...] = acc[1].astype(BF16)


def ring(size, shift):
    return [(i, (i + shift) % size) for i in range(size)]


def gather_weight(block):
    pairs = []
    for a in range(8):
        for b in range(4):
            for c in range(8):
                pairs.append(((a * 4 + b) * 8 + c, (c * 4 + b) * 8 + a))
    first = lax.ppermute(block, ("ylo", "z", "core", "x", "yhi"), pairs)
    second = lax.ppermute(first, "ylo", ring(2, 1))
    blocks, places = [first, second], [(0, 0), (1, 0)]
    up, down = [first, second], [first, second]
    for step in range(1, 5):
        for turn in range(2):
            up[turn] = lax.ppermute(up[turn], "z", ring(8, 1))
            blocks.append(up[turn])
            places.append((turn, 8 - step))
            if step < 4:
                down[turn] = lax.ppermute(down[turn], "z", ring(8, -1))
                blocks.append(down[turn])
                places.append((turn, step))
    return blocks, places


def shards(outer_gate, inner_gate, values, residues, decays, out_weight):
    blocks, places = gather_weight(out_weight)
    tiled = jax.ShapeDtypeStruct((TILES, ROWS, LANES), F32)
    half = jax.ShapeDtypeStruct((MODES, HALF), F32)
    tile_scratch = pltpu.VMEM((TILES, ROWS, LANES), F32)
    work = ROWS * CHANS * MODES * 2
    sums, keep, send = call(
        sums_body, [tiled, half, half], [tile_scratch], work, 1 << 20, inner_gate, values, decays
    )
    core, z, y = lax.axis_index("core"), lax.axis_index("z"), lax.axis_index("ylo")
    came = lax.ppermute(send, "core", ring(2, 1))
    mine = lax.dynamic_slice_in_dim(decays, core * HALF, HALF, 1)
    fade = jnp.exp(-mine * ROWS)
    first = jnp.where(core == 0, keep, came)
    chip = fade * first + jnp.where(core == 0, came, keep)
    everyone = lax.all_to_all(jnp.broadcast_to(chip[None], (16, MODES, HALF)), ("ylo", "z"), 0, 0)
    local = call(
        taps_body, tiled, [tile_scratch], ROWS * CHANS * SUB, 1 << 20, inner_gate, values, residues, decays
    )
    place = y * 8 + z
    chip_fade = fade * fade
    state = jnp.zeros_like(chip)
    for k in range(15):
        state = jnp.where(k < place, state * chip_fade + everyone[k], state)
    after = fade * state + first
    near = jnp.where(core == 0, state, after)
    far = lax.ppermute(jnp.where(core == 0, after, state), "core", ring(2, 1))
    copies = jax.ShapeDtypeStruct((8, ROWS, CHANS), BF16)
    gated = call(
        gate_body, copies, [tile_scratch, tile_scratch], work, 4 << 20,
        outer_gate, sums, local, near, far, residues, decays,
    )
    own = lax.all_to_all(gated, ("x", "yhi"), 0, 0)
    other = lax.ppermute(own, "core", ring(2, 1))
    part = jax.ShapeDtypeStruct((2, ROWS, 256), BF16)
    kept, sent = call(
        lambda *refs: project_body(places, *refs),
        [part, part],
        [pltpu.VMEM((2, 2, ROWS, 256), F32)],
        2 * 512 * 512 * 4096, 10 << 20,
        own, other, *blocks,
    )
    swapped = lax.ppermute(sent, "core", ring(2, 1))
    even = jnp.where(core == 0, kept, swapped)
    odd = jnp.where(core == 0, swapped, kept)
    return jnp.concatenate([even[0], odd[0], even[1], odd[1]], axis=1)


def solution(mesh):
    wide = Mesh(mesh.devices.reshape(2, 8, 2, 4, 2), ("ylo", "z", "core", "x", "yhi"))
    ctx, ch = ("ylo", "z", "core"), ("x", "yhi")
    return jax.shard_map(
        shards,
        mesh=wide,
        in_specs=(P(ctx, ch), P(ctx, ch), P(ctx, ch), P(None, ch), P(None, ch), P(ch, ctx)),
        out_specs=P(ctx, ch),
        check_vma=False,
    )
```

```python
import jax
import jax.numpy as jnp
from jax import lax
from jax.experimental import pallas as pl
from jax.experimental.pallas import tpu as pltpu
from jax.sharding import Mesh
from jax.sharding import PartitionSpec as P

ROWS, CHANS, MODES = 256, 512, 16
SUB = 16
BLOCKS = ROWS // SUB
LANES = 128
TILES = CHANS // LANES
HALF = CHANS // 2
F32, BF16 = jnp.float32, jnp.bfloat16
VMEM_LIMIT = 48 * 1024 * 1024


def whole(n):
    return [pl.BlockSpec(memory_space=pltpu.VMEM)] * n


def call(body, outs, scratch, flops, moved, *args):
    return pl.pallas_call(
        body,
        out_shape=outs,
        in_specs=whole(len(args)),
        out_specs=whole(len(outs)) if isinstance(outs, (list, tuple)) else whole(1)[0],
        scratch_shapes=scratch,
        compiler_params=pltpu.CompilerParams(vmem_limit_bytes=VMEM_LIMIT),
        cost_estimate=pl.CostEstimate(flops=flops, bytes_accessed=moved, transcendentals=0),
    )(*args)


def signal_into(inner, values, sig):
    for lt in range(TILES):
        cols = slice(lt * LANES, (lt + 1) * LANES)
        product = inner[:, cols].astype(F32) * values[:, cols].astype(F32)
        sig[lt] = product.astype(BF16).astype(F32)


def sums_body(inner, values, decays, sums, keep, send, sig):
    signal_into(inner, values, sig)
    for lt in range(TILES):
        cols = slice(lt * LANES, (lt + 1) * LANES)
        fade = jnp.exp(-decays[:, cols])
        for group in range(0, MODES, 8):
            step = [jnp.broadcast_to(fade[r : r + 1], (BLOCKS, LANES)) for r in range(group, group + 8)]
            total = [sig[lt, pl.ds(0, BLOCKS, stride=SUB), :]] * 8
            for b in range(1, SUB):
                row = sig[lt, pl.ds(b, BLOCKS, stride=SUB), :]
                total = [t * e + row for t, e in zip(total, step)]
            for i in range(8):
                sums[lt, pl.ds(group + i, BLOCKS, stride=MODES), :] = total[i]
    core = lax.axis_index("core")
    for lt in range(TILES):
        cols = slice(lt * LANES, (lt + 1) * LANES)
        fade = jnp.exp(-decays[:, cols] * SUB)
        state = sums[lt, 0:MODES, :]
        for a in range(1, BLOCKS):
            state = state * fade + sums[lt, a * MODES : (a + 1) * MODES, :]
        place = slice((lt % 2) * LANES, (lt % 2 + 1) * LANES)

        @pl.when(core == lt // 2)
        def _():
            keep[:, place] = state

        @pl.when(core != lt // 2)
        def _():
            send[:, place] = state


def taps_body(inner, values, residues, decays, local, sig):
    signal_into(inner, values, sig)
    for lt in range(TILES):
        cols = slice(lt * LANES, (lt + 1) * LANES)
        fade = jnp.exp(-decays[:, cols])
        weight = residues[:, cols]
        taps = []
        for lag in range(SUB):
            taps.append(jnp.broadcast_to(jnp.sum(weight, axis=0, keepdims=True), (BLOCKS, LANES)))
            weight = weight * fade
        rows = [sig[lt, pl.ds(b, BLOCKS, stride=SUB), :] for b in range(SUB)]
        for b in range(SUB):
            total = taps[0] * rows[b]
            for lag in range(1, b + 1):
                total = total + taps[lag] * rows[b - lag]
            local[lt, pl.ds(b, BLOCKS, stride=SUB), :] = total


def gate_body(outer, sums, local, near, far, residues, decays, gated, states, out):
    core = lax.axis_index("core")
    for lt in range(TILES):
        cols = slice(lt * LANES, (lt + 1) * LANES)
        place = slice((lt % 2) * LANES, (lt % 2 + 1) * LANES)
        fade = jnp.exp(-decays[:, cols] * SUB)
        weight = residues[:, cols]
        state = jnp.where(core == lt // 2, near[:, place], far[:, place])
        for a in range(BLOCKS):
            states[lt, a * MODES : (a + 1) * MODES, :] = state * weight
            if a + 1 < BLOCKS:
                state = state * fade + sums[lt, a * MODES : (a + 1) * MODES, :]
    for lt in range(TILES):
        cols = slice(lt * LANES, (lt + 1) * LANES)
        fade = jnp.exp(-decays[:, cols])
        step = [jnp.broadcast_to(fade[r : r + 1], (BLOCKS, LANES)) for r in range(MODES)]
        part = [states[lt, pl.ds(r, BLOCKS, stride=MODES), :] for r in range(MODES)]
        for b in range(SUB):
            part = [t * e for t, e in zip(part, step)]
            total = part
            while len(total) > 1:
                total = [total[i] + total[i + 1] for i in range(0, len(total), 2)]
            out[lt, pl.ds(b, BLOCKS, stride=SUB), :] = total[0] + local[lt, pl.ds(b, BLOCKS, stride=SUB), :]
    for lt in range(TILES):
        cols = slice(lt * LANES, (lt + 1) * LANES)
        result = (outer[:, cols].astype(F32) * out[lt]).astype(BF16)
        for copy in range(gated.shape[0]):
            gated[copy, :, cols] = result


def project_body(places, ranks, *refs):
    pieces = refs[: len(ranks)]
    blocks = refs[len(ranks) : len(ranks) + len(places)]
    mine, theirs, gated, weight, acc, piece_sem, block_sem = refs[len(ranks) + len(places) :]
    x, yhi = lax.axis_index("x"), lax.axis_index("yhi")
    z, ylo = lax.axis_index("z"), lax.axis_index("ylo")
    loads = []
    for i, (piece, (rows, dx, dy)) in enumerate(zip(pieces, ranks)):
        rank = lax.rem(x + dx, 4) * 2 + lax.rem(yhi + dy, 2)
        loads.append(pltpu.make_async_copy(piece, gated.at[rows, rank], piece_sem.at[i]))
    stores = [
        pltpu.make_async_copy(block, weight.at[i], block_sem.at[i]) for i, block in enumerate(blocks)
    ]
    for copy in loads + stores:
        copy.start()
    acc[...] = jnp.zeros_like(acc)
    for copy in loads:
        copy.wait()
    for i, (turn, shift) in enumerate(places):
        at = lax.rem(z + shift, 8)
        rank = lax.rem(ylo + turn, 2) * 4 + at // 2
        odd = lax.rem(at, 2)
        stores[i].wait()
        for rows in range(2):
            acc[rows, odd] += jnp.dot(gated[rows, rank], weight[i], preferred_element_type=F32)
    mine[...] = acc[0].astype(BF16)
    theirs[...] = acc[1].astype(BF16)


def ring(size, shift):
    return [(i, (i + shift) % size) for i in range(size)]


def swap(block):
    pairs = []
    for a in range(8):
        for b in range(4):
            for c in range(8):
                pairs.append(((a * 4 + b) * 8 + c, (c * 4 + b) * 8 + a))
    return lax.ppermute(block, ("ylo", "z", "core", "x", "yhi"), pairs)


def move(value, axis, shift):
    return lax.ppermute(value, axis, ring({"ylo": 2, "z": 8, "core": 2, "x": 4, "yhi": 2}[axis], shift))


def together(*values):
    return lax.optimization_barrier(values)


def shards(outer_gate, inner_gate, values, residues, decays, out_weight):
    first = swap(out_weight)
    tiled = jax.ShapeDtypeStruct((TILES, ROWS, LANES), F32)
    half = jax.ShapeDtypeStruct((MODES, HALF), F32)
    tile_scratch = pltpu.VMEM((TILES, ROWS, LANES), F32)
    work = ROWS * CHANS * MODES * 2
    sums, keep, send = call(
        sums_body, [tiled, half, half], [tile_scratch], work, 1 << 20, inner_gate, values, decays
    )
    core, z, y = lax.axis_index("core"), lax.axis_index("z"), lax.axis_index("ylo")
    came = move(send, "core", 1)
    mine = lax.dynamic_slice_in_dim(decays, core * HALF, HALF, 1)
    fade = jnp.exp(-mine * ROWS)
    before = jnp.where(core == 0, keep, came)
    chip = fade * before + jnp.where(core == 0, came, keep)
    everyone = lax.all_to_all(jnp.broadcast_to(chip[None], (16, MODES, HALF)), ("ylo", "z"), 0, 0)
    local = call(
        taps_body, tiled, [tile_scratch], ROWS * CHANS * SUB, 1 << 20, inner_gate, values, residues, decays
    )
    everyone, local, first = together(everyone, local, first)

    second, up_a, down_a = move(first, "ylo", 1), move(first, "z", 1), move(first, "z", -1)
    place = y * 8 + z
    chip_fade = fade * fade
    state = jnp.zeros_like(chip)
    for k in range(15):
        state = jnp.where(k < place, state * chip_fade + everyone[k], state)
    after = fade * state + before
    near = jnp.where(core == 0, state, after)
    far = move(jnp.where(core == 0, after, state), "core", 1)
    gated = call(
        gate_body, jax.ShapeDtypeStruct((1, ROWS, CHANS), BF16), [tile_scratch, tile_scratch], work, 2 << 20,
        outer_gate, sums, local, near, far, residues, decays,
    )
    blocks, places = [first, second, up_a, down_a], [(0, 0), (1, 0), (0, 7), (0, 1)]

    def arrived(*new):
        for block, at in new:
            blocks.append(block)
            places.append(at)

    gated, second, up_a, down_a = together(gated, second, up_a, down_a)
    side = move(gated, "yhi", 1)
    up_a, down_a = move(up_a, "z", 1), move(down_a, "z", -1)
    up_b, down_b = move(second, "z", 1), move(second, "z", -1)
    arrived((up_a, (0, 6)), (down_a, (0, 2)), (up_b, (1, 7)), (down_b, (1, 1)))

    side, up_a, down_a, up_b, down_b = together(side, up_a, down_a, up_b, down_b)
    pair = jnp.concatenate([gated, side], axis=0)
    pair_up, pair_down = move(pair, "x", 1), move(pair, "x", -1)
    up_a, down_a = move(up_a, "z", 1), move(down_a, "z", -1)
    up_b, down_b = move(up_b, "z", 1), move(down_b, "z", -1)
    other = move(pair, "core", 1)
    arrived((up_a, (0, 5)), (down_a, (0, 3)), (up_b, (1, 6)), (down_b, (1, 2)))

    pair_up, pair_down, up_a, up_b, down_b, other = together(pair_up, pair_down, up_a, up_b, down_b, other)
    far_same, far_cross = move(pair_up[0], "x", 1), move(pair_down[1], "x", -1)
    up_a, up_b, down_b = move(up_a, "z", 1), move(up_b, "z", 1), move(down_b, "z", -1)
    other_up, other_down = move(pair_up, "core", 1), move(pair_down, "core", 1)
    arrived((up_a, (0, 4)), (up_b, (1, 5)), (down_b, (1, 3)))

    far_same, far_cross, down_b, other_up, other_down = together(far_same, far_cross, down_b, other_up, other_down)
    down_b = move(down_b, "z", -1)
    other_same, other_cross = move(far_same, "core", 1), move(far_cross, "core", 1)
    arrived((down_b, (1, 4)))

    pieces, ranks = [], []
    for rows, group in enumerate(
        [(pair, pair_up, pair_down, far_same, far_cross), (other, other_up, other_down, other_same, other_cross)]
    ):
        for value, dx in zip(group[:3], (0, 3, 1)):
            for dy in range(2):
                pieces.append(value[dy])
                ranks.append((rows, dx, dy))
        for dy in range(2):
            pieces.append(group[3 + dy])
            ranks.append((rows, 2, dy))
    part = jax.ShapeDtypeStruct((2, ROWS, 256), BF16)
    kept, sent = pl.pallas_call(
        lambda *refs: project_body(places, ranks, *refs),
        out_shape=[part, part],
        in_specs=[pl.BlockSpec(memory_space=pl.ANY)] * (len(pieces) + len(blocks)),
        out_specs=whole(2),
        scratch_shapes=[
            pltpu.VMEM((2, 8, ROWS, CHANS), BF16),
            pltpu.VMEM((len(blocks), 512, 256), BF16),
            pltpu.VMEM((2, 2, ROWS, 256), F32),
            pltpu.SemaphoreType.DMA((len(pieces),)),
            pltpu.SemaphoreType.DMA((len(blocks),)),
        ],
        compiler_params=pltpu.CompilerParams(vmem_limit_bytes=VMEM_LIMIT),
        cost_estimate=pl.CostEstimate(flops=2 * 512 * 512 * 4096, bytes_accessed=10 << 20, transcendentals=0),
    )(*pieces, *blocks)
    swapped = move(sent, "core", 1)
    even = jnp.where(core == 0, kept, swapped)
    odd = jnp.where(core == 0, swapped, kept)
    return jnp.concatenate([even[0], odd[0], even[1], odd[1]], axis=1)


def solution(mesh):
    wide = Mesh(mesh.devices.reshape(2, 8, 2, 4, 2), ("ylo", "z", "core", "x", "yhi"))
    ctx, ch = ("ylo", "z", "core"), ("x", "yhi")
    return jax.shard_map(
        shards,
        mesh=wide,
        in_specs=(P(ctx, ch), P(ctx, ch), P(ctx, ch), P(None, ch), P(None, ch), P(ch, ctx)),
        out_specs=P(ctx, ch),
        check_vma=False,
    )
```

```python
import jax
import jax.numpy as jnp
import numpy as np
from jax import lax
from jax.experimental import pallas as pl
from jax.experimental.pallas import tpu as pltpu
from jax.sharding import Mesh
from jax.sharding import PartitionSpec as P

ROWS, CHANS, MODES = 256, 512, 16
SUB = 16
BLOCKS = ROWS // SUB
LANES = 128
TILES = CHANS // LANES
HALF = CHANS // 2
F32, BF16 = jnp.float32, jnp.bfloat16
VMEM_LIMIT = 48 * 1024 * 1024
AHEAD = 10**11


def whole(n):
    return [pl.BlockSpec(memory_space=pltpu.VMEM)] * n


def call(body, outs, scratch, flops, moved, *args):
    return pl.pallas_call(
        body,
        out_shape=outs,
        in_specs=whole(len(args)),
        out_specs=whole(len(outs)) if isinstance(outs, (list, tuple)) else whole(1)[0],
        scratch_shapes=scratch,
        compiler_params=pltpu.CompilerParams(vmem_limit_bytes=VMEM_LIMIT),
        cost_estimate=pl.CostEstimate(flops=flops, bytes_accessed=moved, transcendentals=0),
    )(*args)


def signal_into(inner, values, sig):
    for lt in range(TILES):
        cols = slice(lt * LANES, (lt + 1) * LANES)
        product = inner[:, cols].astype(F32) * values[:, cols].astype(F32)
        sig[lt] = product.astype(BF16).astype(F32)


def sums_body(inner_hbm, values_hbm, decays_hbm, sums, keep, send, sig, inner, values, decays, sems):
    pairs = ((decays_hbm, decays), (inner_hbm, inner), (values_hbm, values))
    copies = [pltpu.make_async_copy(a, b, sems.at[i]) for i, (a, b) in enumerate(pairs)]
    for copy in copies:
        copy.start()
    for copy in copies:
        copy.wait()
    signal_into(inner, values, sig)
    for lt in range(TILES):
        cols = slice(lt * LANES, (lt + 1) * LANES)
        fade = jnp.exp(-decays[:, cols])
        for group in range(0, MODES, 8):
            step = [jnp.broadcast_to(fade[r : r + 1], (BLOCKS, LANES)) for r in range(group, group + 8)]
            total = [sig[lt, pl.ds(0, BLOCKS, stride=SUB), :]] * 8
            for b in range(1, SUB):
                row = sig[lt, pl.ds(b, BLOCKS, stride=SUB), :]
                total = [t * e + row for t, e in zip(total, step)]
            for i in range(8):
                sums[lt, pl.ds(group + i, BLOCKS, stride=MODES), :] = total[i]
    core = lax.axis_index("core")
    for lt in range(TILES):
        cols = slice(lt * LANES, (lt + 1) * LANES)
        fade = jnp.exp(-decays[:, cols] * SUB)
        state = sums[lt, 0:MODES, :]
        for a in range(1, BLOCKS):
            state = state * fade + sums[lt, a * MODES : (a + 1) * MODES, :]
        place = slice((lt % 2) * LANES, (lt % 2 + 1) * LANES)

        @pl.when(core == lt // 2)
        def _():
            keep[:, place] = state

        @pl.when(core != lt // 2)
        def _():
            send[:, place] = state


def taps_body(inner, values, residues, decays, local, sig):
    signal_into(inner, values, sig)
    for lt in range(TILES):
        cols = slice(lt * LANES, (lt + 1) * LANES)
        fade = jnp.exp(-decays[:, cols])
        weight = residues[:, cols]
        taps = []
        for lag in range(SUB):
            taps.append(jnp.broadcast_to(jnp.sum(weight, axis=0, keepdims=True), (BLOCKS, LANES)))
            weight = weight * fade
        rows = [sig[lt, pl.ds(b, BLOCKS, stride=SUB), :] for b in range(SUB)]
        for b in range(SUB):
            total = taps[0] * rows[b]
            for lag in range(1, b + 1):
                total = total + taps[lag] * rows[b - lag]
            local[lt, pl.ds(b, BLOCKS, stride=SUB), :] = total


def gate_body(outer, sums, local, near, far, residues, decays, gated, states, out):
    core = lax.axis_index("core")
    for lt in range(TILES):
        cols = slice(lt * LANES, (lt + 1) * LANES)
        place = slice((lt % 2) * LANES, (lt % 2 + 1) * LANES)
        fade = jnp.exp(-decays[:, cols] * SUB)
        weight = residues[:, cols]
        state = jnp.where(core == lt // 2, near[:, place], far[:, place])
        for a in range(BLOCKS):
            states[lt, a * MODES : (a + 1) * MODES, :] = state * weight
            if a + 1 < BLOCKS:
                state = state * fade + sums[lt, a * MODES : (a + 1) * MODES, :]
    for lt in range(TILES):
        cols = slice(lt * LANES, (lt + 1) * LANES)
        fade = jnp.exp(-decays[:, cols])
        step = [jnp.broadcast_to(fade[r : r + 1], (BLOCKS, LANES)) for r in range(MODES)]
        part = [states[lt, pl.ds(r, BLOCKS, stride=MODES), :] for r in range(MODES)]
        for b in range(SUB):
            part = [t * e for t, e in zip(part, step)]
            total = part
            while len(total) > 1:
                total = [total[i] + total[i + 1] for i in range(0, len(total), 2)]
            out[lt, pl.ds(b, BLOCKS, stride=SUB), :] = total[0] + local[lt, pl.ds(b, BLOCKS, stride=SUB), :]
    for lt in range(TILES):
        cols = slice(lt * LANES, (lt + 1) * LANES)
        result = (outer[:, cols].astype(F32) * out[lt]).astype(BF16)
        for copy in range(gated.shape[0]):
            gated[copy, :, cols] = result


def source_of(turn, shift):
    x, yhi = lax.axis_index("x"), lax.axis_index("yhi")
    z, ylo = lax.axis_index("z"), lax.axis_index("ylo")
    ahead = lax.rem(z + shift + 8 - 2 * (lax.rem(x, 2) * 2 + yhi), 8)
    odd = jnp.where((ahead >= 1) & (ahead <= 4), 1, 0)
    far = jnp.where(odd == 1, ahead - 1, lax.rem(8 - ahead, 8))
    turned = jnp.where(far == 0, 2, jnp.where(far == 1, 3, jnp.where(far == 2, 1, 0)))
    group = lax.rem(x + turned, 4) * 2 + lax.rem(ylo + turn + yhi, 2)
    return group, odd


def bundle_body(*refs):
    stacks, (out, sems) = refs[:-2], refs[-2:]
    copies, at = [], 0
    for i, stack in enumerate(stacks):
        count = stack.shape[0]
        copies.append(pltpu.make_async_copy(stack, out.at[at : at + count], sems.at[i]))
        at += count
    for copy in copies:
        copy.start()
    for copy in copies:
        copy.wait()


def bundle(stacks):
    count = sum(stack.shape[0] for stack in stacks)
    return pl.pallas_call(
        bundle_body,
        out_shape=jax.ShapeDtypeStruct((count, 512, 256), BF16),
        in_specs=[pl.BlockSpec(memory_space=pl.ANY)] * len(stacks),
        out_specs=pl.BlockSpec(memory_space=pl.ANY),
        scratch_shapes=[pltpu.SemaphoreType.DMA((len(stacks),))],
        compiler_params=pltpu.CompilerParams(vmem_limit_bytes=VMEM_LIMIT),
        cost_estimate=pl.CostEstimate(flops=0, bytes_accessed=count << 19, transcendentals=0),
    )(*stacks)


RANKS = [(dx, dy) for dx in (0, 3, 1, 2) for dy in range(2)]


def project_body(places, counts, *refs):
    pieces, stacks = refs[:8], refs[8 : 8 + len(counts)]
    result, gated, weight, row_sem, block_sem = refs[8 + len(counts) :]
    x, yhi, core = lax.axis_index("x"), lax.axis_index("yhi"), lax.axis_index("core")
    copies = []
    for i, (piece, (dx, dy)) in enumerate(zip(pieces, RANKS)):
        rank = lax.rem(x + dx, 4) * 2 + lax.rem(yhi + dy, 2)
        columns = pl.ds(pl.multiple_of(rank * CHANS, CHANS), CHANS)
        copies.append(pltpu.make_async_copy(piece, gated.at[:, columns], row_sem.at[i]))
    at = 0
    for stack, count in zip(stacks, counts):
        for i in range(count):
            side, (group, odd) = at // 16, source_of(*places[at % 16])
            columns = slice(side * 256, side * 256 + 256)
            copies.append(pltpu.make_async_copy(stack.at[i], weight.at[odd, group, :, columns], block_sem.at[at]))
            at += 1
    for copy in copies:
        copy.start()
    for copy in copies:
        copy.wait()
    for odd in range(2):
        total = jnp.dot(gated[...], weight[odd].reshape(8 * 512, 512), preferred_element_type=F32).astype(BF16)
        own, other = total[:, :256], total[:, 256:]
        result[:, odd * 512 : odd * 512 + 256] = jnp.where(core == 0, own, other)
        result[:, odd * 512 + 256 : odd * 512 + 512] = jnp.where(core == 0, other, own)


def project(places, pieces, stacks):
    counts = [stack.shape[0] for stack in stacks]
    return pl.pallas_call(
        lambda *refs: project_body(places, counts, *refs),
        out_shape=jax.ShapeDtypeStruct((ROWS, 1024), BF16),
        in_specs=[pl.BlockSpec(memory_space=pl.ANY)] * (8 + len(stacks)),
        out_specs=whole(1)[0],
        scratch_shapes=[
            pltpu.VMEM((ROWS, 8 * CHANS), BF16),
            pltpu.VMEM((2, 8, 512, 512), BF16),
            pltpu.SemaphoreType.DMA((8,)),
            pltpu.SemaphoreType.DMA((32,)),
        ],
        compiler_params=pltpu.CompilerParams(vmem_limit_bytes=VMEM_LIMIT),
        cost_estimate=pl.CostEstimate(flops=1 << 31, bytes_accessed=10 << 20, transcendentals=0),
    )(*pieces, *stacks)


def ring(size, shift):
    return [(i, (i + shift) % size) for i in range(size)]


def swap(block):
    def number(x, yhi, ylo, z, core):
        return ((ylo * 8 + z) * 2 + core) * 8 + x * 2 + yhi

    pairs = []
    for x, yhi, ylo, z, core in np.ndindex(4, 2, 2, 8, 2):
        to_x, to_yhi = ylo * 2 + z // 4, z // 2 % 2
        far = (3, 2, 0, 1)[(x - to_x) % 4]
        to_z = (z + far if z % 2 else z - far) % 8
        pairs.append((number(x, yhi, ylo, z, core), number(to_x, to_yhi, yhi ^ to_yhi, to_z, core)))
    return lax.ppermute(block, ("ylo", "z", "core", "x", "yhi"), pairs)


def move(value, axis, shift):
    return lax.ppermute(value, axis, ring({"ylo": 2, "z": 8, "core": 2, "x": 4, "yhi": 2}[axis], shift))


def together(*values):
    return lax.optimization_barrier(values)


def shards(outer_gate, inner_gate, values, residues, decays, out_weight):
    first = swap(out_weight)
    tiled = jax.ShapeDtypeStruct((TILES, ROWS, LANES), F32)
    half = jax.ShapeDtypeStruct((MODES, HALF), F32)
    tile_scratch = pltpu.VMEM((TILES, ROWS, LANES), F32)
    work = ROWS * CHANS * MODES * 2
    shard = pltpu.VMEM((ROWS, CHANS), BF16)
    sums, keep, send = pl.pallas_call(
        sums_body,
        out_shape=[tiled, half, half],
        in_specs=[pl.BlockSpec(memory_space=pl.ANY)] * 3,
        out_specs=whole(3),
        scratch_shapes=[tile_scratch, shard, shard, pltpu.VMEM((MODES, CHANS), F32), pltpu.SemaphoreType.DMA((3,))],
        compiler_params=pltpu.CompilerParams(vmem_limit_bytes=60 * 1024 * 1024),
        cost_estimate=pl.CostEstimate(flops=work, bytes_accessed=1 << 20, transcendentals=0),
    )(inner_gate, values, decays)
    core, z, y = lax.axis_index("core"), lax.axis_index("z"), lax.axis_index("ylo")
    came = move(send, "core", 1)
    mine = lax.dynamic_slice_in_dim(decays, core * HALF, HALF, 1)
    fade = jnp.exp(-mine * ROWS)
    before = jnp.where(core == 0, keep, came)
    chip = fade * before + jnp.where(core == 0, came, keep)
    everyone = lax.all_to_all(jnp.broadcast_to(chip[None], (16, MODES, HALF)), ("ylo", "z"), 0, 0)
    first, late_inner, late_values = together(first, inner_gate, values)
    local = call(
        taps_body, tiled, [tile_scratch], AHEAD, 1 << 20, late_inner, late_values, residues, decays
    )

    first = first[None]
    second, up, down = move(first, "ylo", 1), move(first, "z", 1), move(first, "z", -1)
    everyone, second, up, down = together(everyone, second, up, down)
    early, places = [first, second, up, down], [(0, 0), (1, 0), (0, 7), (0, 1)]
    place = y * 8 + z
    chip_fade = fade * fade
    state = jnp.zeros_like(chip)
    for k in range(15):
        state = jnp.where(k < place, state * chip_fade + everyone[k], state)
    after = fade * state + before
    near = jnp.where(core == 0, state, after)
    far = move(jnp.where(core == 0, after, state), "core", 1)
    gated = call(
        gate_body, jax.ShapeDtypeStruct((1, ROWS, CHANS), BF16), [tile_scratch, tile_scratch], work, 2 << 20,
        outer_gate, sums, local, near, far, residues, decays,
    )
    side = move(gated, "yhi", 1)
    up = move(jnp.concatenate([up, second], axis=0), "z", 1)
    down = move(jnp.concatenate([down, second], axis=0), "z", -1)
    side, up, down = together(side, up, down)
    early, places = early + [up, down], places + [(0, 6), (1, 7), (0, 2), (1, 1)]

    pair = jnp.concatenate([gated, side], axis=0)
    pair_up, pair_down = move(pair, "x", 1), move(pair, "x", -1)
    up, down = move(up, "z", 1), move(down, "z", -1)
    pair_up, pair_down, up, down = together(pair_up, pair_down, up, down)
    early, places = early + [up, down], places + [(0, 5), (1, 6), (0, 3), (1, 2)]

    far_same, far_cross = move(pair_up[0], "x", 1), move(pair_down[1], "x", -1)
    up, down = move(up, "z", 1), move(down[1:], "z", -1)
    far_same, far_cross, up, down, *early = together(far_same, far_cross, up, down, *early)
    last = move(up[:1], "ylo", 1)
    early = bundle(early)
    stacks, places = [early, up, down, last], places + [(0, 4), (1, 5), (1, 3), (1, 4)]
    pieces = [v[dy] for v in (pair, pair_up, pair_down) for dy in range(2)] + [far_same, far_cross]
    return project(places, pieces, stacks + [move(stack, "core", 1) for stack in stacks])


def solution(mesh):
    wide = Mesh(mesh.devices.reshape(2, 8, 2, 4, 2), ("ylo", "z", "core", "x", "yhi"))
    ctx, ch = ("ylo", "z", "core"), ("x", "yhi")
    return jax.shard_map(
        shards,
        mesh=wide,
        in_specs=(P(ctx, ch), P(ctx, ch), P(ctx, ch), P(None, ch), P(None, ch), P(ch, ctx)),
        out_specs=P(ctx, ch),
        check_vma=False,
    )
```

```python
import jax
import jax.numpy as jnp
import numpy as np
from jax import lax
from jax.experimental import pallas as pl
from jax.experimental.pallas import tpu as pltpu
from jax.sharding import Mesh
from jax.sharding import PartitionSpec as P

ROWS, CHANS, MODES = 256, 512, 16
SUB = 16
BLOCKS = ROWS // SUB
LANES = 128
TILES = CHANS // LANES
HALF = CHANS // 2
F32, BF16 = jnp.float32, jnp.bfloat16
VMEM_LIMIT = 24 * 1024 * 1024
AHEAD = 10**11


def whole(n):
    return [pl.BlockSpec(memory_space=pltpu.VMEM)] * n


def call(body, outs, scratch, flops, moved, *args):
    return pl.pallas_call(
        body,
        out_shape=outs,
        in_specs=whole(len(args)),
        out_specs=whole(len(outs)) if isinstance(outs, (list, tuple)) else whole(1)[0],
        scratch_shapes=scratch,
        compiler_params=pltpu.CompilerParams(vmem_limit_bytes=VMEM_LIMIT),
        cost_estimate=pl.CostEstimate(flops=flops, bytes_accessed=moved, transcendentals=0),
    )(*args)


def signal_into(inner, values, sig):
    for lt in range(TILES):
        cols = slice(lt * LANES, (lt + 1) * LANES)
        product = inner[:, cols].astype(F32) * values[:, cols].astype(F32)
        sig[lt] = product.astype(BF16).astype(F32)


def load(sems, *pairs):
    copies = [pltpu.make_async_copy(a, b, sems.at[i]) for i, (a, b) in enumerate(pairs)]
    for copy in copies:
        copy.start()
    for copy in copies:
        copy.wait()


def sums_body(inner_hbm, values_hbm, decays_hbm, sums, keep, send, sig, inner, values, decays, sems):
    load(sems, (decays_hbm, decays), (inner_hbm, inner), (values_hbm, values))
    signal_into(inner, values, sig)
    for lt in range(TILES):
        cols = slice(lt * LANES, (lt + 1) * LANES)
        fade = jnp.exp(-decays[:, cols])
        for group in range(0, MODES, 8):
            step = [jnp.broadcast_to(fade[r : r + 1], (BLOCKS, LANES)) for r in range(group, group + 8)]
            total = [sig[lt, pl.ds(0, BLOCKS, stride=SUB), :]] * 8
            for b in range(1, SUB):
                row = sig[lt, pl.ds(b, BLOCKS, stride=SUB), :]
                total = [t * e + row for t, e in zip(total, step)]
            for i in range(8):
                sums[lt, pl.ds(group + i, BLOCKS, stride=MODES), :] = total[i]
    core = lax.axis_index("core")
    for lt in range(TILES):
        cols = slice(lt * LANES, (lt + 1) * LANES)
        fade = jnp.exp(-decays[:, cols] * SUB)
        state = sums[lt, 0:MODES, :]
        for a in range(1, BLOCKS):
            state = state * fade + sums[lt, a * MODES : (a + 1) * MODES, :]
        place = slice((lt % 2) * LANES, (lt % 2 + 1) * LANES)

        @pl.when(core == lt // 2)
        def _():
            keep[:, place] = state

        @pl.when(core != lt // 2)
        def _():
            send[:, place] = state


def taps_body(inner_hbm, values_hbm, residues_hbm, decays_hbm, local, sig, inner, values, residues, decays, sems):
    load(sems, (inner_hbm, inner), (values_hbm, values), (residues_hbm, residues), (decays_hbm, decays))
    signal_into(inner, values, sig)
    for lt in range(TILES):
        cols = slice(lt * LANES, (lt + 1) * LANES)
        fade = jnp.exp(-decays[:, cols])
        weight = residues[:, cols]
        taps = []
        for lag in range(SUB):
            taps.append(jnp.broadcast_to(jnp.sum(weight, axis=0, keepdims=True), (BLOCKS, LANES)))
            weight = weight * fade
        rows = [sig[lt, pl.ds(b, BLOCKS, stride=SUB), :] for b in range(SUB)]
        for b in range(SUB):
            total = taps[0] * rows[b]
            for lag in range(1, b + 1):
                total = total + taps[lag] * rows[b - lag]
            local[lt, pl.ds(b, BLOCKS, stride=SUB), :] = total


def gate_body(outer, sums, local, near, far, residues, decays, gated, states, out):
    core = lax.axis_index("core")
    for lt in range(TILES):
        cols = slice(lt * LANES, (lt + 1) * LANES)
        place = slice((lt % 2) * LANES, (lt % 2 + 1) * LANES)
        fade = jnp.exp(-decays[:, cols] * SUB)
        weight = residues[:, cols]
        state = jnp.where(core == lt // 2, near[:, place], far[:, place])
        for a in range(BLOCKS):
            states[lt, a * MODES : (a + 1) * MODES, :] = state * weight
            if a + 1 < BLOCKS:
                state = state * fade + sums[lt, a * MODES : (a + 1) * MODES, :]
    for lt in range(TILES):
        cols = slice(lt * LANES, (lt + 1) * LANES)
        fade = jnp.exp(-decays[:, cols])
        step = [jnp.broadcast_to(fade[r : r + 1], (BLOCKS, LANES)) for r in range(MODES)]
        part = [states[lt, pl.ds(r, BLOCKS, stride=MODES), :] for r in range(MODES)]
        for b in range(SUB):
            part = [t * e for t, e in zip(part, step)]
            total = part
            while len(total) > 1:
                total = [total[i] + total[i + 1] for i in range(0, len(total), 2)]
            out[lt, pl.ds(b, BLOCKS, stride=SUB), :] = total[0] + local[lt, pl.ds(b, BLOCKS, stride=SUB), :]
    for lt in range(TILES):
        cols = slice(lt * LANES, (lt + 1) * LANES)
        result = (outer[:, cols].astype(F32) * out[lt]).astype(BF16)
        for copy in range(gated.shape[0]):
            gated[copy, :, cols] = result


def source_of(turn, shift):
    x, yhi = lax.axis_index("x"), lax.axis_index("yhi")
    z, ylo = lax.axis_index("z"), lax.axis_index("ylo")
    ahead = lax.rem(z + shift + 8 - 2 * (lax.rem(x, 2) * 2 + yhi), 8)
    odd = jnp.where((ahead >= 1) & (ahead <= 4), 1, 0)
    far = jnp.where(odd == 1, ahead - 1, lax.rem(8 - ahead, 8))
    turned = jnp.where(far == 0, 2, jnp.where(far == 1, 3, jnp.where(far == 2, 1, 0)))
    group = lax.rem(x + turned, 4) * 2 + lax.rem(ylo + turn + yhi, 2)
    return group, odd


def bundle_body(*refs):
    stacks, (out, sems) = refs[:-2], refs[-2:]
    copies, at = [], 0
    for i, stack in enumerate(stacks):
        count = stack.shape[0]
        copies.append(pltpu.make_async_copy(stack, out.at[at : at + count], sems.at[i]))
        at += count
    for copy in copies:
        copy.start()
    for copy in copies:
        copy.wait()


def bundle(stacks, cost=0):
    count = sum(stack.shape[0] for stack in stacks)
    return pl.pallas_call(
        bundle_body,
        out_shape=jax.ShapeDtypeStruct((count, 512, 256), BF16),
        in_specs=[pl.BlockSpec(memory_space=pl.ANY)] * len(stacks),
        out_specs=pl.BlockSpec(memory_space=pl.ANY),
        scratch_shapes=[pltpu.SemaphoreType.DMA((len(stacks),))],
        compiler_params=pltpu.CompilerParams(vmem_limit_bytes=VMEM_LIMIT),
        cost_estimate=pl.CostEstimate(flops=cost, bytes_accessed=count << 19, transcendentals=0),
    )(*stacks)


RANKS = [(dx, dy) for dx in (0, 3, 1, 2) for dy in range(2)]


LAST = (1, 4)


def project_body(places, counts, *refs):
    pieces, stacks = refs[:8], refs[8 : 8 + len(counts)]
    total, rows, gated, weight, row_sem, block_sem = refs[8 + len(counts) :]
    x, yhi = lax.axis_index("x"), lax.axis_index("yhi")
    copies = []
    for i, (piece, (dx, dy)) in enumerate(zip(pieces, RANKS)):
        rank = lax.rem(x + dx, 4) * 2 + lax.rem(yhi + dy, 2)
        columns = pl.ds(pl.multiple_of(rank * CHANS, CHANS), CHANS)
        copies.append(pltpu.make_async_copy(piece, gated.at[:, columns], row_sem.at[i]))
    at = 0
    for stack, count in zip(stacks, counts):
        for i in range(count):
            side, (group, odd) = at // 15, source_of(*places[at % 15])
            columns = slice(side * 256, side * 256 + 256)
            copies.append(pltpu.make_async_copy(stack.at[i], weight.at[odd, group, :, columns], block_sem.at[at]))
            at += 1
    for copy in copies:
        copy.start()
    group, odd = source_of(*LAST)
    weight[odd, group] = jnp.zeros((512, 512), BF16)
    for copy in copies:
        copy.wait()
    rows[...] = gated[:, pl.ds(pl.multiple_of(group * CHANS, CHANS), CHANS)]
    for odd in range(2):
        total[odd] = jnp.dot(gated[...], weight[odd].reshape(8 * 512, 512), preferred_element_type=F32)


def project(places, pieces, stacks):
    counts = [stack.shape[0] for stack in stacks]
    return pl.pallas_call(
        lambda *refs: project_body(places, counts, *refs),
        out_shape=[jax.ShapeDtypeStruct((2, ROWS, 512), F32), jax.ShapeDtypeStruct((ROWS, CHANS), BF16)],
        in_specs=[pl.BlockSpec(memory_space=pl.ANY)] * (8 + len(stacks)),
        out_specs=whole(2),
        scratch_shapes=[
            pltpu.VMEM((ROWS, 8 * CHANS), BF16),
            pltpu.VMEM((2, 8, 512, 512), BF16),
            pltpu.SemaphoreType.DMA((8,)),
            pltpu.SemaphoreType.DMA((30,)),
        ],
        compiler_params=pltpu.CompilerParams(vmem_limit_bytes=VMEM_LIMIT),
        cost_estimate=pl.CostEstimate(flops=1 << 31, bytes_accessed=10 << 20, transcendentals=0),
    )(*pieces, *stacks)


def finish_body(total, rows, own, other, result):
    core = lax.axis_index("core")
    _, odd = source_of(*LAST)
    parts = [jnp.dot(rows[...], side[0], preferred_element_type=F32) for side in (own, other)]
    for half in range(2):
        mine, theirs = (
            (total[half, :, i * 256 : i * 256 + 256] + jnp.where(odd == half, parts[i], 0.0)).astype(BF16)
            for i in range(2)
        )
        result[:, half * 512 : half * 512 + 256] = jnp.where(core == 0, mine, theirs)
        result[:, half * 512 + 256 : half * 512 + 512] = jnp.where(core == 0, theirs, mine)


def ring(size, shift):
    return [(i, (i + shift) % size) for i in range(size)]


def swap(block):
    def number(x, yhi, ylo, z, core):
        return ((ylo * 8 + z) * 2 + core) * 8 + x * 2 + yhi

    pairs = []
    for x, yhi, ylo, z, core in np.ndindex(4, 2, 2, 8, 2):
        to_x, to_yhi = ylo * 2 + z // 4, z // 2 % 2
        far = (3, 2, 0, 1)[(x - to_x) % 4]
        to_z = (z + far if z % 2 else z - far) % 8
        pairs.append((number(x, yhi, ylo, z, core), number(to_x, to_yhi, yhi ^ to_yhi, to_z, core)))
    return lax.ppermute(block, ("ylo", "z", "core", "x", "yhi"), pairs)


def move(value, axis, shift):
    return lax.ppermute(value, axis, ring({"ylo": 2, "z": 8, "core": 2, "x": 4, "yhi": 2}[axis], shift))


def together(*values):
    return lax.optimization_barrier(values)


def shards(outer_gate, inner_gate, values, residues, decays, out_weight):
    first = swap(out_weight)
    tiled = jax.ShapeDtypeStruct((TILES, ROWS, LANES), F32)
    half = jax.ShapeDtypeStruct((MODES, HALF), F32)
    tile_scratch = pltpu.VMEM((TILES, ROWS, LANES), F32)
    work = ROWS * CHANS * MODES * 2
    shard, modes = pltpu.VMEM((ROWS, CHANS), BF16), pltpu.VMEM((MODES, CHANS), F32)
    full = pltpu.CompilerParams(vmem_limit_bytes=60 * 1024 * 1024)
    sums, keep, send = pl.pallas_call(
        sums_body,
        out_shape=[tiled, half, half],
        in_specs=[pl.BlockSpec(memory_space=pl.ANY)] * 3,
        out_specs=whole(3),
        scratch_shapes=[tile_scratch, shard, shard, modes, pltpu.SemaphoreType.DMA((3,))],
        compiler_params=full,
        cost_estimate=pl.CostEstimate(flops=work, bytes_accessed=2 << 20, transcendentals=0),
    )(inner_gate, values, decays)
    core, z, y = lax.axis_index("core"), lax.axis_index("z"), lax.axis_index("ylo")
    came = move(send, "core", 1)
    mine = lax.dynamic_slice_in_dim(decays, core * HALF, HALF, 1)
    fade = jnp.exp(-mine * ROWS)
    before = jnp.where(core == 0, keep, came)
    chip = fade * before + jnp.where(core == 0, came, keep)
    everyone = lax.all_to_all(jnp.broadcast_to(chip[None], (16, MODES, HALF)), ("ylo", "z"), 0, 0)
    first, late_inner = together(first, inner_gate)
    local = pl.pallas_call(
        taps_body,
        out_shape=tiled,
        in_specs=[pl.BlockSpec(memory_space=pl.ANY)] * 4,
        out_specs=whole(1)[0],
        scratch_shapes=[tile_scratch, shard, shard, modes, modes, pltpu.SemaphoreType.DMA((4,))],
        compiler_params=full,
        cost_estimate=pl.CostEstimate(flops=AHEAD, bytes_accessed=1 << 20, transcendentals=0),
    )(late_inner, values, residues, decays)
    chip_fade = fade * fade
    first = first[None]
    second, up_a, down_a = move(first, "ylo", 1), move(first, "z", 1), move(first, "z", -1)
    early, places = [first, second, up_a, down_a], [(0, 0), (1, 0), (0, 7), (0, 1)]
    place = y * 8 + z
    state = jnp.zeros_like(chip)
    for k in range(15):
        state = jnp.where(k < place, state * chip_fade + everyone[k], state)
    after = fade * state + before
    near = jnp.where(core == 0, state, after)
    far = move(jnp.where(core == 0, after, state), "core", 1)
    gated = call(
        gate_body, jax.ShapeDtypeStruct((1, ROWS, CHANS), BF16), [tile_scratch, tile_scratch], work, 2 << 20,
        outer_gate, sums, local, near, far, residues, decays,
    )
    gated, second, up_a, down_a = together(gated, second, up_a, down_a)
    early = [first, second, up_a, down_a]
    up_b, down_b = move(second, "z", 1), move(second, "z", -1)
    up_a, down_a = move(up_a, "z", 1), move(down_a, "z", -1)
    early, places = early + [up_a, up_b, down_a, down_b], places + [(0, 6), (1, 7), (0, 2), (1, 1)]
    side = move(gated, "yhi", 1)
    side, *early = together(side, *early)
    early = bundle(early)

    up_a, down_a = move(up_a, "z", 1), move(down_a, "z", -1)
    up_b, down_b = move(up_b, "z", 1), move(down_b, "z", -1)
    late, places = [up_a, down_a, up_b, down_b], places + [(0, 5), (0, 3), (1, 6), (1, 2)]
    pair = jnp.concatenate([gated, side], axis=0)
    pair_up, pair_down = move(pair, "x", 1), move(pair, "x", -1)
    pair_up, pair_down, _, _, _, _, early = together(pair_up, pair_down, up_a, down_a, up_b, down_b, early)

    far_same, far_cross = move(pair_up[0], "x", 1), move(pair_down[1], "x", -1)
    side_a, up_a, down_b = move(up_a, "ylo", 1), move(up_a, "z", 1), move(down_b, "z", -1)
    last = move(up_a, "ylo", 1)
    far_same, far_cross, up_a, side_a, down_b = together(far_same, far_cross, up_a, side_a, down_b)
    late, places = bundle(late + [up_a, side_a, down_b], AHEAD), places + [(0, 4), (1, 5), (1, 3)]
    pieces = [v[dy] for v in (pair, pair_up, pair_down) for dy in range(2)] + [far_same, far_cross]
    total, rows = project(places, pieces, [early, late, move(early, "core", 1), move(late, "core", 1)])
    last, total = together(last, total)
    return call(
        finish_body, jax.ShapeDtypeStruct((ROWS, 1024), BF16), [], 1 << 27, 2 << 20,
        total, rows, last, move(last, "core", 1),
    )


def solution(mesh):
    wide = Mesh(mesh.devices.reshape(2, 8, 2, 4, 2), ("ylo", "z", "core", "x", "yhi"))
    ctx, ch = ("ylo", "z", "core"), ("x", "yhi")
    return jax.shard_map(
        shards,
        mesh=wide,
        in_specs=(P(ctx, ch), P(ctx, ch), P(ctx, ch), P(None, ch), P(None, ch), P(ch, ctx)),
        out_specs=P(ctx, ch),
        check_vma=False,
    )
```

```python
import jax
import jax.numpy as jnp
import numpy as np
from jax import lax
from jax.experimental import pallas as pl
from jax.experimental.pallas import tpu as pltpu
from jax.sharding import Mesh
from jax.sharding import PartitionSpec as P

ROWS, CHANS, MODES = 256, 512, 16
SUB = 16
BLOCKS = ROWS // SUB
LANES = 128
TILES = CHANS // LANES
HALF = CHANS // 2
F32, BF16 = jnp.float32, jnp.bfloat16
VMEM_LIMIT = 24 * 1024 * 1024
AHEAD = 10**11


def whole(n):
    return [pl.BlockSpec(memory_space=pltpu.VMEM)] * n


def call(body, outs, scratch, flops, moved, *args):
    return pl.pallas_call(
        body,
        out_shape=outs,
        in_specs=whole(len(args)),
        out_specs=whole(len(outs)) if isinstance(outs, (list, tuple)) else whole(1)[0],
        scratch_shapes=scratch,
        compiler_params=pltpu.CompilerParams(vmem_limit_bytes=VMEM_LIMIT),
        cost_estimate=pl.CostEstimate(flops=flops, bytes_accessed=moved, transcendentals=0),
    )(*args)


def signal_into(inner, values, sig):
    for lt in range(TILES):
        cols = slice(lt * LANES, (lt + 1) * LANES)
        product = inner[:, cols].astype(F32) * values[:, cols].astype(F32)
        sig[lt] = product.astype(BF16).astype(F32)


def load(sems, *pairs):
    copies = [pltpu.make_async_copy(a, b, sems.at[i]) for i, (a, b) in enumerate(pairs)]
    for copy in copies:
        copy.start()
    for copy in copies:
        copy.wait()


def sums_body(inner_hbm, values_hbm, decays_hbm, sums, keep, send, sig, inner, values, decays, sems):
    load(sems, (decays_hbm, decays), (inner_hbm, inner), (values_hbm, values))
    signal_into(inner, values, sig)
    for lt in range(TILES):
        cols = slice(lt * LANES, (lt + 1) * LANES)
        fade = jnp.exp(-decays[:, cols])
        for group in range(0, MODES, 8):
            step = [jnp.broadcast_to(fade[r : r + 1], (BLOCKS, LANES)) for r in range(group, group + 8)]
            total = [sig[lt, pl.ds(0, BLOCKS, stride=SUB), :]] * 8
            for b in range(1, SUB):
                row = sig[lt, pl.ds(b, BLOCKS, stride=SUB), :]
                total = [t * e + row for t, e in zip(total, step)]
            for i in range(8):
                sums[lt, pl.ds(group + i, BLOCKS, stride=MODES), :] = total[i]
    core = lax.axis_index("core")
    for lt in range(TILES):
        cols = slice(lt * LANES, (lt + 1) * LANES)
        fade = jnp.exp(-decays[:, cols] * SUB)
        state = sums[lt, 0:MODES, :]
        for a in range(1, BLOCKS):
            state = state * fade + sums[lt, a * MODES : (a + 1) * MODES, :]
        place = slice((lt % 2) * LANES, (lt % 2 + 1) * LANES)

        @pl.when(core == lt // 2)
        def _():
            keep[:, place] = state

        @pl.when(core != lt // 2)
        def _():
            send[:, place] = state


def taps_body(inner_hbm, values_hbm, residues_hbm, decays_hbm, local, sig, inner, values, residues, decays, sems):
    load(sems, (inner_hbm, inner), (values_hbm, values), (residues_hbm, residues), (decays_hbm, decays))
    signal_into(inner, values, sig)
    for lt in range(TILES):
        cols = slice(lt * LANES, (lt + 1) * LANES)
        fade = jnp.exp(-decays[:, cols])
        weight = residues[:, cols]
        taps = []
        for lag in range(SUB):
            taps.append(jnp.broadcast_to(jnp.sum(weight, axis=0, keepdims=True), (BLOCKS, LANES)))
            weight = weight * fade
        rows = [sig[lt, pl.ds(b, BLOCKS, stride=SUB), :] for b in range(SUB)]
        for b in range(SUB):
            total = taps[0] * rows[b]
            for lag in range(1, b + 1):
                total = total + taps[lag] * rows[b - lag]
            local[lt, pl.ds(b, BLOCKS, stride=SUB), :] = total


def gate_body(outer, sums, local, near, far, residues, decays, gated, states, out):
    core = lax.axis_index("core")
    for lt in range(TILES):
        cols = slice(lt * LANES, (lt + 1) * LANES)
        place = slice((lt % 2) * LANES, (lt % 2 + 1) * LANES)
        fade = jnp.exp(-decays[:, cols] * SUB)
        weight = residues[:, cols]
        state = jnp.where(core == lt // 2, near[:, place], far[:, place])
        for a in range(BLOCKS):
            states[lt, a * MODES : (a + 1) * MODES, :] = state * weight
            if a + 1 < BLOCKS:
                state = state * fade + sums[lt, a * MODES : (a + 1) * MODES, :]
    for lt in range(TILES):
        cols = slice(lt * LANES, (lt + 1) * LANES)
        fade = jnp.exp(-decays[:, cols])
        step = [jnp.broadcast_to(fade[r : r + 1], (BLOCKS, LANES)) for r in range(MODES)]
        part = [states[lt, pl.ds(r, BLOCKS, stride=MODES), :] for r in range(MODES)]
        for b in range(SUB):
            part = [t * e for t, e in zip(part, step)]
            total = part
            while len(total) > 1:
                total = [total[i] + total[i + 1] for i in range(0, len(total), 2)]
            out[lt, pl.ds(b, BLOCKS, stride=SUB), :] = total[0] + local[lt, pl.ds(b, BLOCKS, stride=SUB), :]
    for lt in range(TILES):
        cols = slice(lt * LANES, (lt + 1) * LANES)
        result = (outer[:, cols].astype(F32) * out[lt]).astype(BF16)
        for copy in range(gated.shape[0]):
            gated[copy, :, cols] = result


def source_of(turn, shift):
    x, yhi = lax.axis_index("x"), lax.axis_index("yhi")
    z, ylo = lax.axis_index("z"), lax.axis_index("ylo")
    ahead = lax.rem(z + shift + 8 - 2 * (lax.rem(x, 2) * 2 + yhi), 8)
    odd = jnp.where((ahead >= 1) & (ahead <= 4), 1, 0)
    far = jnp.where(odd == 1, ahead - 1, lax.rem(8 - ahead, 8))
    turned = jnp.where(far == 0, 2, jnp.where(far == 1, 3, jnp.where(far == 2, 1, 0)))
    group = lax.rem(x + turned, 4) * 2 + lax.rem(ylo + turn + yhi, 2)
    return group, odd


def bundle_body(*refs):
    stacks, (out, sems) = refs[:-2], refs[-2:]
    copies, at = [], 0
    for i, stack in enumerate(stacks):
        count = stack.shape[0]
        copies.append(pltpu.make_async_copy(stack, out.at[at : at + count], sems.at[i]))
        at += count
    for copy in copies:
        copy.start()
    for copy in copies:
        copy.wait()


def bundle(stacks, cost=0):
    count = sum(stack.shape[0] for stack in stacks)
    return pl.pallas_call(
        bundle_body,
        out_shape=jax.ShapeDtypeStruct((count, 512, 256), BF16),
        in_specs=[pl.BlockSpec(memory_space=pl.ANY)] * len(stacks),
        out_specs=pl.BlockSpec(memory_space=pl.ANY),
        scratch_shapes=[pltpu.SemaphoreType.DMA((len(stacks),))],
        compiler_params=pltpu.CompilerParams(vmem_limit_bytes=VMEM_LIMIT),
        cost_estimate=pl.CostEstimate(flops=cost, bytes_accessed=count << 19, transcendentals=0),
    )(*stacks)


RANKS = [(dx, dy) for dx in (0, 3, 1, 2) for dy in range(2)]


def column_sums(places, stacks, gated, weight, sems):
    copies = []
    for stack in stacks:
        for i in range(stack.shape[0]):
            at = len(copies)
            group, odd = source_of(*places[at])
            copies.append(pltpu.make_async_copy(stack.at[i], weight.at[odd, group], sems.at[at]))
    for copy in copies:
        copy.start()
    for copy in copies:
        copy.wait()
    return [jnp.dot(gated[...], weight[odd].reshape(8 * 512, 256), preferred_element_type=F32) for odd in range(2)]


def own_body(places, count, *refs):
    pieces, stacks = refs[:8], refs[8 : 8 + count]
    total, gated, weight, row_sem, block_sem = refs[8 + count :]
    x, yhi = lax.axis_index("x"), lax.axis_index("yhi")
    copies = []
    for i, (piece, (dx, dy)) in enumerate(zip(pieces, RANKS)):
        rank = lax.rem(x + dx, 4) * 2 + lax.rem(yhi + dy, 2)
        columns = pl.ds(pl.multiple_of(rank * CHANS, CHANS), CHANS)
        copies.append(pltpu.make_async_copy(piece, gated.at[:, columns], row_sem.at[i]))
    for copy in copies:
        copy.start()
    for copy in copies:
        copy.wait()
    total[0], total[1] = column_sums(places, stacks, gated, weight, block_sem)


def other_body(places, count, *refs):
    total, gated, stacks = refs[0], refs[1], refs[2 : 2 + count]
    result, weight, block_sem = refs[2 + count :]
    core = lax.axis_index("core")
    for odd, theirs in enumerate(column_sums(places, stacks, gated, weight, block_sem)):
        mine, theirs = total[odd].astype(BF16), theirs.astype(BF16)
        result[:, odd * 512 : odd * 512 + 256] = jnp.where(core == 0, mine, theirs)
        result[:, odd * 512 + 256 : odd * 512 + 512] = jnp.where(core == 0, theirs, mine)


def project(places, pieces, own, other):
    blocks = [pltpu.VMEM((2, 8, 512, 256), BF16)]
    sems = [pltpu.SemaphoreType.DMA((16,))]
    params = pltpu.CompilerParams(vmem_limit_bytes=VMEM_LIMIT)
    cost = pl.CostEstimate(flops=1 << 30, bytes_accessed=6 << 20, transcendentals=0)
    total, gated = pl.pallas_call(
        lambda *refs: own_body(places, len(own), *refs),
        out_shape=[jax.ShapeDtypeStruct((2, ROWS, 256), F32), jax.ShapeDtypeStruct((ROWS, 8 * CHANS), BF16)],
        in_specs=[pl.BlockSpec(memory_space=pl.ANY)] * (8 + len(own)),
        out_specs=whole(2),
        scratch_shapes=blocks + [pltpu.SemaphoreType.DMA((8,))] + sems,
        compiler_params=params,
        cost_estimate=cost,
    )(*pieces, *own)
    return pl.pallas_call(
        lambda *refs: other_body(places, len(other), *refs),
        out_shape=jax.ShapeDtypeStruct((ROWS, 1024), BF16),
        in_specs=whole(2) + [pl.BlockSpec(memory_space=pl.ANY)] * len(other),
        out_specs=whole(1)[0],
        scratch_shapes=blocks + sems,
        compiler_params=params,
        cost_estimate=cost,
    )(total, gated, *other)


def ring(size, shift):
    return [(i, (i + shift) % size) for i in range(size)]


def swap(block):
    def number(x, yhi, ylo, z, core):
        return ((ylo * 8 + z) * 2 + core) * 8 + x * 2 + yhi

    pairs = []
    for x, yhi, ylo, z, core in np.ndindex(4, 2, 2, 8, 2):
        to_x, to_yhi = ylo * 2 + z // 4, z // 2 % 2
        far = (3, 2, 0, 1)[(x - to_x) % 4]
        to_z = (z + far if z % 2 else z - far) % 8
        pairs.append((number(x, yhi, ylo, z, core), number(to_x, to_yhi, yhi ^ to_yhi, to_z, core)))
    return lax.ppermute(block, ("ylo", "z", "core", "x", "yhi"), pairs)


def move(value, axis, shift):
    return lax.ppermute(value, axis, ring({"ylo": 2, "z": 8, "core": 2, "x": 4, "yhi": 2}[axis], shift))


def together(*values):
    return lax.optimization_barrier(values)


def shards(outer_gate, inner_gate, values, residues, decays, out_weight):
    first = swap(out_weight)
    tiled = jax.ShapeDtypeStruct((TILES, ROWS, LANES), F32)
    half = jax.ShapeDtypeStruct((MODES, HALF), F32)
    tile_scratch = pltpu.VMEM((TILES, ROWS, LANES), F32)
    work = ROWS * CHANS * MODES * 2
    shard, modes = pltpu.VMEM((ROWS, CHANS), BF16), pltpu.VMEM((MODES, CHANS), F32)
    full = pltpu.CompilerParams(vmem_limit_bytes=60 * 1024 * 1024)
    sums, keep, send = pl.pallas_call(
        sums_body,
        out_shape=[tiled, half, half],
        in_specs=[pl.BlockSpec(memory_space=pl.ANY)] * 3,
        out_specs=whole(3),
        scratch_shapes=[tile_scratch, shard, shard, modes, pltpu.SemaphoreType.DMA((3,))],
        compiler_params=full,
        cost_estimate=pl.CostEstimate(flops=work, bytes_accessed=2 << 20, transcendentals=0),
    )(inner_gate, values, decays)
    core, z, y = lax.axis_index("core"), lax.axis_index("z"), lax.axis_index("ylo")
    came = move(send, "core", 1)
    mine = lax.dynamic_slice_in_dim(decays, core * HALF, HALF, 1)
    fade = jnp.exp(-mine * ROWS)
    before = jnp.where(core == 0, keep, came)
    chip = fade * before + jnp.where(core == 0, came, keep)
    everyone = lax.all_to_all(jnp.broadcast_to(chip[None], (16, MODES, HALF)), ("ylo", "z"), 0, 0)
    first, late_inner = together(first, inner_gate)
    local = pl.pallas_call(
        taps_body,
        out_shape=tiled,
        in_specs=[pl.BlockSpec(memory_space=pl.ANY)] * 4,
        out_specs=whole(1)[0],
        scratch_shapes=[tile_scratch, shard, shard, modes, modes, pltpu.SemaphoreType.DMA((4,))],
        compiler_params=pltpu.CompilerParams(vmem_limit_bytes=VMEM_LIMIT),
        cost_estimate=pl.CostEstimate(flops=AHEAD, bytes_accessed=1 << 20, transcendentals=0),
    )(late_inner, values, residues, decays)
    chip_fade = fade * fade
    first = first[None]
    second, up_a, down_a = move(first, "ylo", 1), move(first, "z", 1), move(first, "z", -1)
    early, places = [first, second, up_a, down_a], [(0, 0), (1, 0), (0, 7), (0, 1)]
    place = y * 8 + z
    state = jnp.zeros_like(chip)
    for k in range(15):
        state = jnp.where(k < place, state * chip_fade + everyone[k], state)
    after = fade * state + before
    near = jnp.where(core == 0, state, after)
    far = move(jnp.where(core == 0, after, state), "core", 1)
    gated = call(
        gate_body, jax.ShapeDtypeStruct((1, ROWS, CHANS), BF16), [tile_scratch, tile_scratch], 0, 0,
        outer_gate, sums, local, near, far, residues, decays,
    )
    gated, second, up_a, down_a = together(gated, second, up_a, down_a)
    early = [first, second, up_a, down_a]
    near_b = [move(second, "z", 1), move(second, "z", -1)]
    up_a, down_a = move(up_a, "z", 1), move(down_a, "z", -1)
    early, places = early + [up_a, down_a], places + [(0, 6), (0, 2)]
    side = move(gated, "yhi", 1)
    side, *early = together(side, *early)
    early = bundle(early)

    up_b, down_b = move(up_a, "ylo", 1), move(down_a, "ylo", 1)
    up_a, down_a = move(up_a, "z", 1), move(down_a, "z", -1)
    opposite = move(up_a, "z", 1)
    middle, places = [up_a, down_a, up_b, down_b, opposite], places + [(0, 5), (0, 3), (1, 6), (1, 2), (0, 4)]
    middle, places = middle + near_b, places + [(1, 7), (1, 1)]
    pair = jnp.concatenate([gated, side], axis=0)
    pair_up, pair_down = move(pair, "x", 1), move(pair, "x", -1)
    pair_up, pair_down, early, *middle = together(pair_up, pair_down, early, *middle)

    far_same, far_cross = move(pair_up[0], "x", 1), move(pair_down[1], "x", -1)
    late = [move(up_b, "z", 1), move(down_b, "z", -1), move(opposite, "ylo", 1)]
    places += [(1, 5), (1, 3), (1, 4)]
    far_same, far_cross, *late = together(far_same, far_cross, *late)
    pieces = [v[dy] for v in (pair, pair_up, pair_down) for dy in range(2)] + [far_same, far_cross]
    stacks = [early, bundle(middle + late)]
    return project(places, pieces, stacks, [move(stack, "core", 1) for stack in stacks])


def solution(mesh):
    wide = Mesh(mesh.devices.reshape(2, 8, 2, 4, 2), ("ylo", "z", "core", "x", "yhi"))
    ctx, ch = ("ylo", "z", "core"), ("x", "yhi")
    return jax.shard_map(
        shards,
        mesh=wide,
        in_specs=(P(ctx, ch), P(ctx, ch), P(ctx, ch), P(None, ch), P(None, ch), P(ch, ctx)),
        out_specs=P(ctx, ch),
        check_vma=False,
    )
```

```python
import jax
import jax.numpy as jnp
import numpy as np
from jax import lax
from jax.experimental import pallas as pl
from jax.experimental.pallas import tpu as pltpu
from jax.sharding import Mesh
from jax.sharding import PartitionSpec as P

ROWS, CHANS, MODES = 256, 512, 16
SUB = 16
BLOCKS = ROWS // SUB
LANES = 128
TILES = CHANS // LANES
HALF = CHANS // 2
F32, BF16 = jnp.float32, jnp.bfloat16
VMEM_LIMIT = 24 * 1024 * 1024
AHEAD = 10**11


def whole(n):
    return [pl.BlockSpec(memory_space=pltpu.VMEM)] * n


def call(body, outs, scratch, flops, moved, *args):
    return pl.pallas_call(
        body,
        out_shape=outs,
        in_specs=whole(len(args)),
        out_specs=whole(len(outs)) if isinstance(outs, (list, tuple)) else whole(1)[0],
        scratch_shapes=scratch,
        compiler_params=pltpu.CompilerParams(vmem_limit_bytes=VMEM_LIMIT),
        cost_estimate=pl.CostEstimate(flops=flops, bytes_accessed=moved, transcendentals=0),
    )(*args)


def signal_into(inner, values, sig):
    for lt in range(TILES):
        cols = slice(lt * LANES, (lt + 1) * LANES)
        product = inner[:, cols].astype(F32) * values[:, cols].astype(F32)
        sig[lt] = product.astype(BF16).astype(F32)


def load(sems, *pairs):
    copies = [pltpu.make_async_copy(a, b, sems.at[i]) for i, (a, b) in enumerate(pairs)]
    for copy in copies:
        copy.start()
    for copy in copies:
        copy.wait()


def sums_body(inner_hbm, values_hbm, decays_hbm, sums, keep, send, sig, inner, values, decays, sems):
    load(sems, (decays_hbm, decays), (inner_hbm, inner), (values_hbm, values))
    signal_into(inner, values, sig)
    for lt in range(TILES):
        cols = slice(lt * LANES, (lt + 1) * LANES)
        fade = jnp.exp(-decays[:, cols])
        for group in range(0, MODES, 8):
            step = [jnp.broadcast_to(fade[r : r + 1], (BLOCKS, LANES)) for r in range(group, group + 8)]
            total = [sig[lt, pl.ds(0, BLOCKS, stride=SUB), :]] * 8
            for b in range(1, SUB):
                row = sig[lt, pl.ds(b, BLOCKS, stride=SUB), :]
                total = [t * e + row for t, e in zip(total, step)]
            for i in range(8):
                sums[lt, pl.ds(group + i, BLOCKS, stride=MODES), :] = total[i]
    core = lax.axis_index("core")
    for lt in range(TILES):
        cols = slice(lt * LANES, (lt + 1) * LANES)
        fade = jnp.exp(-decays[:, cols] * SUB)
        state = sums[lt, 0:MODES, :]
        for a in range(1, BLOCKS):
            state = state * fade + sums[lt, a * MODES : (a + 1) * MODES, :]
        place = slice((lt % 2) * LANES, (lt % 2 + 1) * LANES)

        @pl.when(core == lt // 2)
        def _():
            keep[:, place] = state

        @pl.when(core != lt // 2)
        def _():
            send[:, place] = state


def taps_body(inner_hbm, values_hbm, residues_hbm, decays_hbm, local, sig, inner, values, residues, decays, sems):
    load(sems, (inner_hbm, inner), (values_hbm, values), (residues_hbm, residues), (decays_hbm, decays))
    signal_into(inner, values, sig)
    for lt in range(TILES):
        cols = slice(lt * LANES, (lt + 1) * LANES)
        fade = jnp.exp(-decays[:, cols])
        weight = residues[:, cols]
        taps = []
        for lag in range(SUB):
            taps.append(jnp.broadcast_to(jnp.sum(weight, axis=0, keepdims=True), (BLOCKS, LANES)))
            weight = weight * fade
        rows = [sig[lt, pl.ds(b, BLOCKS, stride=SUB), :] for b in range(SUB)]
        for b in range(SUB):
            total = taps[0] * rows[b]
            for lag in range(1, b + 1):
                total = total + taps[lag] * rows[b - lag]
            local[lt, pl.ds(b, BLOCKS, stride=SUB), :] = total


def gate_body(outer, sums, local, near, far, residues, decays, gated, states, out):
    core = lax.axis_index("core")
    for lt in range(TILES):
        cols = slice(lt * LANES, (lt + 1) * LANES)
        place = slice((lt % 2) * LANES, (lt % 2 + 1) * LANES)
        fade = jnp.exp(-decays[:, cols] * SUB)
        weight = residues[:, cols]
        state = jnp.where(core == lt // 2, near[:, place], far[:, place])
        for a in range(BLOCKS):
            states[lt, a * MODES : (a + 1) * MODES, :] = state * weight
            if a + 1 < BLOCKS:
                state = state * fade + sums[lt, a * MODES : (a + 1) * MODES, :]
    for lt in range(TILES):
        cols = slice(lt * LANES, (lt + 1) * LANES)
        fade = jnp.exp(-decays[:, cols])
        step = [jnp.broadcast_to(fade[r : r + 1], (BLOCKS, LANES)) for r in range(MODES)]
        part = [states[lt, pl.ds(r, BLOCKS, stride=MODES), :] for r in range(MODES)]
        for b in range(SUB):
            part = [t * e for t, e in zip(part, step)]
            total = part
            while len(total) > 1:
                total = [total[i] + total[i + 1] for i in range(0, len(total), 2)]
            out[lt, pl.ds(b, BLOCKS, stride=SUB), :] = total[0] + local[lt, pl.ds(b, BLOCKS, stride=SUB), :]
    for lt in range(TILES):
        cols = slice(lt * LANES, (lt + 1) * LANES)
        result = (outer[:, cols].astype(F32) * out[lt]).astype(BF16)
        for copy in range(gated.shape[0]):
            gated[copy, :, cols] = result


def source_of(turn, shift):
    x, yhi = lax.axis_index("x"), lax.axis_index("yhi")
    z, ylo = lax.axis_index("z"), lax.axis_index("ylo")
    ahead = lax.rem(z + shift + 8 - 2 * (lax.rem(x, 2) * 2 + yhi), 8)
    odd = jnp.where((ahead >= 1) & (ahead <= 4), 1, 0)
    far = jnp.where(odd == 1, ahead - 1, lax.rem(8 - ahead, 8))
    turned = jnp.where(far == 0, 2, jnp.where(far == 1, 3, jnp.where(far == 2, 1, 0)))
    group = lax.rem(x + turned, 4) * 2 + lax.rem(ylo + turn + yhi, 2)
    return group, odd


def bundle_body(*refs):
    stacks, (out, sems) = refs[:-2], refs[-2:]
    copies, at = [], 0
    for i, stack in enumerate(stacks):
        count = stack.shape[0]
        copies.append(pltpu.make_async_copy(stack, out.at[at : at + count], sems.at[i]))
        at += count
    for copy in copies:
        copy.start()
    for copy in copies:
        copy.wait()


def bundle(stacks, cost=0):
    count = sum(stack.shape[0] for stack in stacks)
    return pl.pallas_call(
        bundle_body,
        out_shape=jax.ShapeDtypeStruct((count, 512, 256), BF16),
        in_specs=[pl.BlockSpec(memory_space=pl.ANY)] * len(stacks),
        out_specs=pl.BlockSpec(memory_space=pl.ANY),
        scratch_shapes=[pltpu.SemaphoreType.DMA((len(stacks),))],
        compiler_params=pltpu.CompilerParams(vmem_limit_bytes=VMEM_LIMIT),
        cost_estimate=pl.CostEstimate(flops=cost, bytes_accessed=count << 19, transcendentals=0),
    )(*stacks)


RANKS = [(dx, dy) for dx in (0, 3, 1, 2) for dy in range(2)]


def column_sums(places, stacks, gated, weight, sems):
    copies = []
    for stack in stacks:
        for i in range(stack.shape[0]):
            at = len(copies)
            group, odd = source_of(*places[at])
            copies.append(pltpu.make_async_copy(stack.at[i], weight.at[odd, group], sems.at[at]))
    for copy in copies:
        copy.start()
    for copy in copies:
        copy.wait()
    return [jnp.dot(gated[...], weight[odd].reshape(8 * 512, 256), preferred_element_type=F32) for odd in range(2)]


def own_body(places, count, *refs):
    pieces, stacks = refs[:8], refs[8 : 8 + count]
    total, gated, weight, row_sem, block_sem = refs[8 + count :]
    x, yhi = lax.axis_index("x"), lax.axis_index("yhi")
    copies = []
    for i, (piece, (dx, dy)) in enumerate(zip(pieces, RANKS)):
        rank = lax.rem(x + dx, 4) * 2 + lax.rem(yhi + dy, 2)
        columns = pl.ds(pl.multiple_of(rank * CHANS, CHANS), CHANS)
        copies.append(pltpu.make_async_copy(piece, gated.at[:, columns], row_sem.at[i]))
    for copy in copies:
        copy.start()
    for copy in copies:
        copy.wait()
    total[0], total[1] = column_sums(places, stacks, gated, weight, block_sem)


def other_body(places, count, *refs):
    total, gated, stacks = refs[0], refs[1], refs[2 : 2 + count]
    result, weight, block_sem = refs[2 + count :]
    core = lax.axis_index("core")
    for odd, theirs in enumerate(column_sums(places, stacks, gated, weight, block_sem)):
        mine, theirs = total[odd].astype(BF16), theirs.astype(BF16)
        result[:, odd * 512 : odd * 512 + 256] = jnp.where(core == 0, mine, theirs)
        result[:, odd * 512 + 256 : odd * 512 + 512] = jnp.where(core == 0, theirs, mine)


def project(places, pieces, own, other):
    blocks = [pltpu.VMEM((2, 8, 512, 256), BF16)]
    sems = [pltpu.SemaphoreType.DMA((16,))]
    params = pltpu.CompilerParams(vmem_limit_bytes=VMEM_LIMIT)
    cost = pl.CostEstimate(flops=1 << 36, bytes_accessed=6 << 20, transcendentals=0)
    total, gated = pl.pallas_call(
        lambda *refs: own_body(places, len(own), *refs),
        out_shape=[jax.ShapeDtypeStruct((2, ROWS, 256), F32), jax.ShapeDtypeStruct((ROWS, 8 * CHANS), BF16)],
        in_specs=[pl.BlockSpec(memory_space=pl.ANY)] * (8 + len(own)),
        out_specs=whole(2),
        scratch_shapes=blocks + [pltpu.SemaphoreType.DMA((8,))] + sems,
        compiler_params=params,
        cost_estimate=cost,
    )(*pieces, *own)
    return pl.pallas_call(
        lambda *refs: other_body(places, len(other), *refs),
        out_shape=jax.ShapeDtypeStruct((ROWS, 1024), BF16),
        in_specs=whole(2) + [pl.BlockSpec(memory_space=pl.ANY)] * len(other),
        out_specs=whole(1)[0],
        scratch_shapes=blocks + sems,
        compiler_params=params,
        cost_estimate=cost,
    )(total, gated, *other)


def ring(size, shift):
    return [(i, (i + shift) % size) for i in range(size)]


def swap(block):
    def number(x, yhi, ylo, z, core):
        return ((ylo * 8 + z) * 2 + core) * 8 + x * 2 + yhi

    pairs = []
    for x, yhi, ylo, z, core in np.ndindex(4, 2, 2, 8, 2):
        to_x, to_yhi = ylo * 2 + z // 4, z // 2 % 2
        far = (3, 2, 0, 1)[(x - to_x) % 4]
        to_z = (z + far if z % 2 else z - far) % 8
        pairs.append((number(x, yhi, ylo, z, core), number(to_x, to_yhi, yhi ^ to_yhi, to_z, core)))
    return lax.ppermute(block, ("ylo", "z", "core", "x", "yhi"), pairs)


def move(value, axis, shift):
    return lax.ppermute(value, axis, ring({"ylo": 2, "z": 8, "core": 2, "x": 4, "yhi": 2}[axis], shift))


def together(*values):
    return lax.optimization_barrier(values)


def shards(outer_gate, inner_gate, values, residues, decays, out_weight):
    first = swap(out_weight)
    tiled = jax.ShapeDtypeStruct((TILES, ROWS, LANES), F32)
    half = jax.ShapeDtypeStruct((MODES, HALF), F32)
    tile_scratch = pltpu.VMEM((TILES, ROWS, LANES), F32)
    work = ROWS * CHANS * MODES * 2
    shard, modes = pltpu.VMEM((ROWS, CHANS), BF16), pltpu.VMEM((MODES, CHANS), F32)
    full = pltpu.CompilerParams(vmem_limit_bytes=60 * 1024 * 1024)
    sums, keep, send = pl.pallas_call(
        sums_body,
        out_shape=[tiled, half, half],
        in_specs=[pl.BlockSpec(memory_space=pl.ANY)] * 3,
        out_specs=whole(3),
        scratch_shapes=[tile_scratch, shard, shard, modes, pltpu.SemaphoreType.DMA((3,))],
        compiler_params=full,
        cost_estimate=pl.CostEstimate(flops=work, bytes_accessed=2 << 20, transcendentals=0),
    )(inner_gate, values, decays)
    core, z, y = lax.axis_index("core"), lax.axis_index("z"), lax.axis_index("ylo")
    came = move(send, "core", 1)
    mine = lax.dynamic_slice_in_dim(decays, core * HALF, HALF, 1)
    fade = jnp.exp(-mine * ROWS)
    before = jnp.where(core == 0, keep, came)
    chip = fade * before + jnp.where(core == 0, came, keep)
    everyone = lax.all_to_all(jnp.broadcast_to(chip[None], (16, MODES, HALF)), ("ylo", "z"), 0, 0)
    first, late_inner = together(first, inner_gate)
    local = pl.pallas_call(
        taps_body,
        out_shape=tiled,
        in_specs=[pl.BlockSpec(memory_space=pl.ANY)] * 4,
        out_specs=whole(1)[0],
        scratch_shapes=[tile_scratch, shard, shard, modes, modes, pltpu.SemaphoreType.DMA((4,))],
        compiler_params=pltpu.CompilerParams(vmem_limit_bytes=VMEM_LIMIT),
        cost_estimate=pl.CostEstimate(flops=AHEAD, bytes_accessed=1 << 20, transcendentals=0),
    )(late_inner, values, residues, decays)
    chip_fade = fade * fade
    first = first[None]
    second, up_a, down_a = move(first, "ylo", 1), move(first, "z", 1), move(first, "z", -1)
    early, places = [first, second, up_a, down_a], [(0, 0), (1, 0), (0, 7), (0, 1)]
    place = y * 8 + z
    state = jnp.zeros_like(chip)
    for k in range(15):
        state = jnp.where(k < place, state * chip_fade + everyone[k], state)
    after = fade * state + before
    near = jnp.where(core == 0, state, after)
    far = move(jnp.where(core == 0, after, state), "core", 1)
    gated = call(
        gate_body, jax.ShapeDtypeStruct((1, ROWS, CHANS), BF16), [tile_scratch, tile_scratch], 0, 0,
        outer_gate, sums, local, near, far, residues, decays,
    )
    gated, second, up_a, down_a = together(gated, second, up_a, down_a)
    early = [first, second, up_a, down_a]
    near_b = [move(second, "z", 1), move(second, "z", -1)]
    up_a, down_a = move(up_a, "z", 1), move(down_a, "z", -1)
    early, places = early + [up_a, down_a], places + [(0, 6), (0, 2)]
    side = move(gated, "yhi", 1)
    side, *early = together(side, *early)
    early = bundle(early, 1 << 36)

    up_b, down_b = move(up_a, "ylo", 1), move(down_a, "ylo", 1)
    up_a, down_a = move(up_a, "z", 1), move(down_a, "z", -1)
    opposite = move(up_a, "z", 1)
    middle, places = [up_a, down_a, up_b, down_b, opposite], places + [(0, 5), (0, 3), (1, 6), (1, 2), (0, 4)]
    middle, places = middle + near_b, places + [(1, 7), (1, 1)]
    pair = jnp.concatenate([gated, side], axis=0)
    pair_up, pair_down = move(pair, "x", 1), move(pair, "x", -1)
    pair_up, pair_down, early, *middle = together(pair_up, pair_down, early, *middle)

    far_same, far_cross = move(pair_up[0], "x", 1), move(pair_down[1], "x", -1)
    late = [move(up_b, "z", 1), move(down_b, "z", -1), move(opposite, "ylo", 1)]
    places += [(1, 5), (1, 3), (1, 4)]
    far_same, far_cross, *late = together(far_same, far_cross, *late)
    pieces = [v[dy] for v in (pair, pair_up, pair_down) for dy in range(2)] + [far_same, far_cross]
    stacks = [early, bundle(middle + late)]
    return project(places, pieces, stacks, [move(stack, "core", 1) for stack in stacks])


def solution(mesh):
    wide = Mesh(mesh.devices.reshape(2, 8, 2, 4, 2), ("ylo", "z", "core", "x", "yhi"))
    ctx, ch = ("ylo", "z", "core"), ("x", "yhi")
    return jax.shard_map(
        shards,
        mesh=wide,
        in_specs=(P(ctx, ch), P(ctx, ch), P(ctx, ch), P(None, ch), P(None, ch), P(ch, ctx)),
        out_specs=P(ctx, ch),
        check_vma=False,
    )
```

```python
import jax
import jax.numpy as jnp
import numpy as np
from jax import lax
from jax.experimental import pallas as pl
from jax.experimental.pallas import tpu as pltpu
from jax.sharding import Mesh
from jax.sharding import PartitionSpec as P

ROWS, CHANS, MODES = 256, 512, 16
SUB = 16
BLOCKS = ROWS // SUB
LANES = 128
TILES = CHANS // LANES
HALF = CHANS // 2
F32, BF16 = jnp.float32, jnp.bfloat16
VMEM_LIMIT = 24 * 1024 * 1024
AHEAD = 10**11


def whole(n):
    return [pl.BlockSpec(memory_space=pltpu.VMEM)] * n


def call(body, outs, scratch, flops, moved, *args):
    return pl.pallas_call(
        body,
        out_shape=outs,
        in_specs=whole(len(args)),
        out_specs=whole(len(outs)) if isinstance(outs, (list, tuple)) else whole(1)[0],
        scratch_shapes=scratch,
        compiler_params=pltpu.CompilerParams(vmem_limit_bytes=VMEM_LIMIT),
        cost_estimate=pl.CostEstimate(flops=flops, bytes_accessed=moved, transcendentals=0),
    )(*args)


def signal_into(inner, values, sig):
    for lt in range(TILES):
        cols = slice(lt * LANES, (lt + 1) * LANES)
        product = inner[:, cols].astype(F32) * values[:, cols].astype(F32)
        sig[lt] = product.astype(BF16).astype(F32)


def load(sems, *pairs):
    copies = [pltpu.make_async_copy(a, b, sems.at[i]) for i, (a, b) in enumerate(pairs)]
    for copy in copies:
        copy.start()
    for copy in copies:
        copy.wait()


def sums_body(inner_hbm, values_hbm, decays_hbm, sums, keep, send, sig, inner, values, decays, sems):
    load(sems, (decays_hbm, decays), (inner_hbm, inner), (values_hbm, values))
    signal_into(inner, values, sig)
    for lt in range(TILES):
        cols = slice(lt * LANES, (lt + 1) * LANES)
        fade = jnp.exp(-decays[:, cols])
        for group in range(0, MODES, 8):
            step = [jnp.broadcast_to(fade[r : r + 1], (BLOCKS, LANES)) for r in range(group, group + 8)]
            total = [sig[lt, pl.ds(0, BLOCKS, stride=SUB), :]] * 8
            for b in range(1, SUB):
                row = sig[lt, pl.ds(b, BLOCKS, stride=SUB), :]
                total = [t * e + row for t, e in zip(total, step)]
            for i in range(8):
                sums[lt, pl.ds(group + i, BLOCKS, stride=MODES), :] = total[i]
    core = lax.axis_index("core")
    for lt in range(TILES):
        cols = slice(lt * LANES, (lt + 1) * LANES)
        fade = jnp.exp(-decays[:, cols] * SUB)
        state = sums[lt, 0:MODES, :]
        for a in range(1, BLOCKS):
            state = state * fade + sums[lt, a * MODES : (a + 1) * MODES, :]
        place = slice((lt % 2) * LANES, (lt % 2 + 1) * LANES)

        @pl.when(core == lt // 2)
        def _():
            keep[:, place] = state

        @pl.when(core != lt // 2)
        def _():
            send[:, place] = state


def taps_body(inner_hbm, values_hbm, residues_hbm, decays_hbm, local, sig, inner, values, residues, decays, sems):
    load(sems, (inner_hbm, inner), (values_hbm, values), (residues_hbm, residues), (decays_hbm, decays))
    signal_into(inner, values, sig)
    for lt in range(TILES):
        cols = slice(lt * LANES, (lt + 1) * LANES)
        fade = jnp.exp(-decays[:, cols])
        weight = residues[:, cols]
        taps = []
        for lag in range(SUB):
            taps.append(jnp.broadcast_to(jnp.sum(weight, axis=0, keepdims=True), (BLOCKS, LANES)))
            weight = weight * fade
        rows = [sig[lt, pl.ds(b, BLOCKS, stride=SUB), :] for b in range(SUB)]
        for b in range(SUB):
            total = taps[0] * rows[b]
            for lag in range(1, b + 1):
                total = total + taps[lag] * rows[b - lag]
            local[lt, pl.ds(b, BLOCKS, stride=SUB), :] = total


def gate_body(outer, sums, local, near, far, residues, decays, gated, states, out):
    core = lax.axis_index("core")
    for lt in range(TILES):
        cols = slice(lt * LANES, (lt + 1) * LANES)
        place = slice((lt % 2) * LANES, (lt % 2 + 1) * LANES)
        fade = jnp.exp(-decays[:, cols] * SUB)
        weight = residues[:, cols]
        state = jnp.where(core == lt // 2, near[:, place], far[:, place])
        for a in range(BLOCKS):
            states[lt, a * MODES : (a + 1) * MODES, :] = state * weight
            if a + 1 < BLOCKS:
                state = state * fade + sums[lt, a * MODES : (a + 1) * MODES, :]
    for lt in range(TILES):
        cols = slice(lt * LANES, (lt + 1) * LANES)
        fade = jnp.exp(-decays[:, cols])
        step = [jnp.broadcast_to(fade[r : r + 1], (BLOCKS, LANES)) for r in range(MODES)]
        part = [states[lt, pl.ds(r, BLOCKS, stride=MODES), :] for r in range(MODES)]
        for b in range(SUB):
            part = [t * e for t, e in zip(part, step)]
            total = part
            while len(total) > 1:
                total = [total[i] + total[i + 1] for i in range(0, len(total), 2)]
            out[lt, pl.ds(b, BLOCKS, stride=SUB), :] = total[0] + local[lt, pl.ds(b, BLOCKS, stride=SUB), :]
    for lt in range(TILES):
        cols = slice(lt * LANES, (lt + 1) * LANES)
        result = (outer[:, cols].astype(F32) * out[lt]).astype(BF16)
        for copy in range(gated.shape[0]):
            gated[copy, :, cols] = result


def source_of(turn, shift):
    x, yhi = lax.axis_index("x"), lax.axis_index("yhi")
    z, ylo = lax.axis_index("z"), lax.axis_index("ylo")
    ahead = lax.rem(z + shift + 8 - 2 * (lax.rem(x, 2) * 2 + yhi), 8)
    odd = jnp.where((ahead >= 1) & (ahead <= 4), 1, 0)
    far = jnp.where(odd == 1, ahead - 1, lax.rem(8 - ahead, 8))
    turned = jnp.where(far == 0, 2, jnp.where(far == 1, 3, jnp.where(far == 2, 1, 0)))
    group = lax.rem(x + turned, 4) * 2 + lax.rem(ylo + turn + yhi, 2)
    return group, odd


def bundle_body(*refs):
    stacks, (out, sems) = refs[:-2], refs[-2:]
    copies, at = [], 0
    for i, stack in enumerate(stacks):
        count = stack.shape[0]
        copies.append(pltpu.make_async_copy(stack, out.at[at : at + count], sems.at[i]))
        at += count
    for copy in copies:
        copy.start()
    for copy in copies:
        copy.wait()


def bundle(stacks, cost=0):
    count = sum(stack.shape[0] for stack in stacks)
    return pl.pallas_call(
        bundle_body,
        out_shape=jax.ShapeDtypeStruct((count, 512, 256), BF16),
        in_specs=[pl.BlockSpec(memory_space=pl.ANY)] * len(stacks),
        out_specs=pl.BlockSpec(memory_space=pl.ANY),
        scratch_shapes=[pltpu.SemaphoreType.DMA((len(stacks),))],
        compiler_params=pltpu.CompilerParams(vmem_limit_bytes=VMEM_LIMIT),
        cost_estimate=pl.CostEstimate(flops=cost, bytes_accessed=count << 19, transcendentals=0),
    )(*stacks)


RANKS = [(dx, dy) for dx in (0, 3, 1, 2) for dy in range(2)]


def column_sums(places, stacks, gated, weight, sems):
    copies = []
    for stack in stacks:
        for i in range(stack.shape[0]):
            at = len(copies)
            group, odd = source_of(*places[at])
            copies.append(pltpu.make_async_copy(stack.at[i], weight.at[odd, group], sems.at[at]))
    for copy in copies:
        copy.start()
    for copy in copies:
        copy.wait()
    return [jnp.dot(gated[...], weight[odd].reshape(8 * 512, 256), preferred_element_type=F32) for odd in range(2)]


def own_body(places, count, *refs):
    pieces, stacks = refs[:8], refs[8 : 8 + count]
    total, gated, weight, row_sem, block_sem = refs[8 + count :]
    x, yhi = lax.axis_index("x"), lax.axis_index("yhi")
    copies = []
    for i, (piece, (dx, dy)) in enumerate(zip(pieces, RANKS)):
        rank = lax.rem(x + dx, 4) * 2 + lax.rem(yhi + dy, 2)
        columns = pl.ds(pl.multiple_of(rank * CHANS, CHANS), CHANS)
        copies.append(pltpu.make_async_copy(piece, gated.at[:, columns], row_sem.at[i]))
    for copy in copies:
        copy.start()
    for copy in copies:
        copy.wait()
    total[0], total[1] = column_sums(places, stacks, gated, weight, block_sem)


def other_body(places, count, *refs):
    total, gated, stacks = refs[0], refs[1], refs[2 : 2 + count]
    result, weight, block_sem = refs[2 + count :]
    core = lax.axis_index("core")
    for odd, theirs in enumerate(column_sums(places, stacks, gated, weight, block_sem)):
        mine, theirs = total[odd].astype(BF16), theirs.astype(BF16)
        result[:, odd * 512 : odd * 512 + 256] = jnp.where(core == 0, mine, theirs)
        result[:, odd * 512 + 256 : odd * 512 + 512] = jnp.where(core == 0, theirs, mine)


def project(places, pieces, own, other):
    blocks = [pltpu.VMEM((2, 8, 512, 256), BF16)]
    sems = [pltpu.SemaphoreType.DMA((16,))]
    params = pltpu.CompilerParams(vmem_limit_bytes=VMEM_LIMIT)
    cost = pl.CostEstimate(flops=1 << 35, bytes_accessed=6 << 20, transcendentals=0)
    total, gated = pl.pallas_call(
        lambda *refs: own_body(places, len(own), *refs),
        out_shape=[jax.ShapeDtypeStruct((2, ROWS, 256), F32), jax.ShapeDtypeStruct((ROWS, 8 * CHANS), BF16)],
        in_specs=[pl.BlockSpec(memory_space=pl.ANY)] * (8 + len(own)),
        out_specs=whole(2),
        scratch_shapes=blocks + [pltpu.SemaphoreType.DMA((8,))] + sems,
        compiler_params=params,
        cost_estimate=cost,
    )(*pieces, *own)
    return pl.pallas_call(
        lambda *refs: other_body(places, len(other), *refs),
        out_shape=jax.ShapeDtypeStruct((ROWS, 1024), BF16),
        in_specs=whole(2) + [pl.BlockSpec(memory_space=pl.ANY)] * len(other),
        out_specs=whole(1)[0],
        scratch_shapes=blocks + sems,
        compiler_params=params,
        cost_estimate=cost,
    )(total, gated, *other)


def ring(size, shift):
    return [(i, (i + shift) % size) for i in range(size)]


def swap(block):
    def number(x, yhi, ylo, z, core):
        return ((ylo * 8 + z) * 2 + core) * 8 + x * 2 + yhi

    pairs = []
    for x, yhi, ylo, z, core in np.ndindex(4, 2, 2, 8, 2):
        to_x, to_yhi = ylo * 2 + z // 4, z // 2 % 2
        far = (3, 2, 0, 1)[(x - to_x) % 4]
        to_z = (z + far if z % 2 else z - far) % 8
        pairs.append((number(x, yhi, ylo, z, core), number(to_x, to_yhi, yhi ^ to_yhi, to_z, core)))
    return lax.ppermute(block, ("ylo", "z", "core", "x", "yhi"), pairs)


def move(value, axis, shift):
    return lax.ppermute(value, axis, ring({"ylo": 2, "z": 8, "core": 2, "x": 4, "yhi": 2}[axis], shift))


def together(*values):
    return lax.optimization_barrier(values)


def shards(outer_gate, inner_gate, values, residues, decays, out_weight):
    first = swap(out_weight)
    tiled = jax.ShapeDtypeStruct((TILES, ROWS, LANES), F32)
    half = jax.ShapeDtypeStruct((MODES, HALF), F32)
    tile_scratch = pltpu.VMEM((TILES, ROWS, LANES), F32)
    work = ROWS * CHANS * MODES * 2
    shard, modes = pltpu.VMEM((ROWS, CHANS), BF16), pltpu.VMEM((MODES, CHANS), F32)
    full = pltpu.CompilerParams(vmem_limit_bytes=60 * 1024 * 1024)
    sums, keep, send = pl.pallas_call(
        sums_body,
        out_shape=[tiled, half, half],
        in_specs=[pl.BlockSpec(memory_space=pl.ANY)] * 3,
        out_specs=whole(3),
        scratch_shapes=[tile_scratch, shard, shard, modes, pltpu.SemaphoreType.DMA((3,))],
        compiler_params=full,
        cost_estimate=pl.CostEstimate(flops=work, bytes_accessed=2 << 20, transcendentals=0),
    )(inner_gate, values, decays)
    core, z, y = lax.axis_index("core"), lax.axis_index("z"), lax.axis_index("ylo")
    came = move(send, "core", 1)
    mine = lax.dynamic_slice_in_dim(decays, core * HALF, HALF, 1)
    fade = jnp.exp(-mine * ROWS)
    before = jnp.where(core == 0, keep, came)
    chip = fade * before + jnp.where(core == 0, came, keep)
    everyone = lax.all_to_all(jnp.broadcast_to(chip[None], (16, MODES, HALF)), ("ylo", "z"), 0, 0)
    first, late_inner = together(first, inner_gate)
    local = pl.pallas_call(
        taps_body,
        out_shape=tiled,
        in_specs=[pl.BlockSpec(memory_space=pl.ANY)] * 4,
        out_specs=whole(1)[0],
        scratch_shapes=[tile_scratch, shard, shard, modes, modes, pltpu.SemaphoreType.DMA((4,))],
        compiler_params=pltpu.CompilerParams(vmem_limit_bytes=VMEM_LIMIT),
        cost_estimate=pl.CostEstimate(flops=AHEAD, bytes_accessed=1 << 20, transcendentals=0),
    )(late_inner, values, residues, decays)
    chip_fade = fade * fade
    first = first[None]
    second, up_a, down_a = move(first, "ylo", 1), move(first, "z", 1), move(first, "z", -1)
    early, places = [first, second, up_a, down_a], [(0, 0), (1, 0), (0, 7), (0, 1)]
    place = y * 8 + z
    state = jnp.zeros_like(chip)
    for k in range(15):
        state = jnp.where(k < place, state * chip_fade + everyone[k], state)
    after = fade * state + before
    near = jnp.where(core == 0, state, after)
    far = move(jnp.where(core == 0, after, state), "core", 1)
    gated = call(
        gate_body, jax.ShapeDtypeStruct((1, ROWS, CHANS), BF16), [tile_scratch, tile_scratch], 0, 0,
        outer_gate, sums, local, near, far, residues, decays,
    )
    gated, second, up_a, down_a = together(gated, second, up_a, down_a)
    early = [first, second, up_a, down_a]
    near_b = [move(second, "z", 1), move(second, "z", -1)]
    up_a, down_a = move(up_a, "z", 1), move(down_a, "z", -1)
    early, places = early + [up_a, down_a], places + [(0, 6), (0, 2)]
    side = move(gated, "yhi", 1)
    side, *early = together(side, *early)
    early = bundle(early, 1 << 36)

    up_b, down_b = move(up_a, "ylo", 1), move(down_a, "ylo", 1)
    up_a, down_a = move(up_a, "z", 1), move(down_a, "z", -1)
    opposite = move(up_a, "z", 1)
    middle, places = [up_a, down_a, up_b, down_b, opposite], places + [(0, 5), (0, 3), (1, 6), (1, 2), (0, 4)]
    middle, places = middle + near_b, places + [(1, 7), (1, 1)]
    pair = jnp.concatenate([gated, side], axis=0)
    pair_up, pair_down = move(pair, "x", 1), move(pair, "x", -1)
    pair_up, pair_down, early, *middle = together(pair_up, pair_down, early, *middle)

    far_same, far_cross = move(pair_up[0], "x", 1), move(pair_down[1], "x", -1)
    late = [move(up_b, "z", 1), move(down_b, "z", -1), move(opposite, "ylo", 1)]
    places += [(1, 5), (1, 3), (1, 4)]
    far_same, far_cross, *late = together(far_same, far_cross, *late)
    pieces = [v[dy] for v in (pair, pair_up, pair_down) for dy in range(2)] + [far_same, far_cross]
    stacks = [early, bundle(middle, 1 << 36), bundle(late)]
    return project(places, pieces, stacks, [move(stack, "core", 1) for stack in stacks])


def solution(mesh):
    wide = Mesh(mesh.devices.reshape(2, 8, 2, 4, 2), ("ylo", "z", "core", "x", "yhi"))
    ctx, ch = ("ylo", "z", "core"), ("x", "yhi")
    return jax.shard_map(
        shards,
        mesh=wide,
        in_specs=(P(ctx, ch), P(ctx, ch), P(ctx, ch), P(None, ch), P(None, ch), P(ch, ctx)),
        out_specs=P(ctx, ch),
        check_vma=False,
    )
```

```python
import jax
import jax.numpy as jnp
import numpy as np
from jax import lax
from jax.experimental import pallas as pl
from jax.experimental.pallas import tpu as pltpu
from jax.sharding import Mesh
from jax.sharding import PartitionSpec as P

ROWS, CHANS, MODES = 256, 512, 16
SUB = 16
BLOCKS = ROWS // SUB
LANES = 128
TILES = CHANS // LANES
HALF = CHANS // 2
F32, BF16 = jnp.float32, jnp.bfloat16
VMEM_LIMIT = 24 * 1024 * 1024
AHEAD = 10**11


def whole(n):
    return [pl.BlockSpec(memory_space=pltpu.VMEM)] * n


def call(body, outs, scratch, flops, moved, *args):
    return pl.pallas_call(
        body,
        out_shape=outs,
        in_specs=whole(len(args)),
        out_specs=whole(len(outs)) if isinstance(outs, (list, tuple)) else whole(1)[0],
        scratch_shapes=scratch,
        compiler_params=pltpu.CompilerParams(vmem_limit_bytes=VMEM_LIMIT),
        cost_estimate=pl.CostEstimate(flops=flops, bytes_accessed=moved, transcendentals=0),
    )(*args)


def signal_tile(inner, values, sig, lt):
    cols = slice(lt * LANES, (lt + 1) * LANES)
    product = inner[:, cols].astype(F32) * values[:, cols].astype(F32)
    sig[lt] = product.astype(BF16).astype(F32)


def signal_into(inner, values, sig):
    for lt in range(TILES):
        signal_tile(inner, values, sig, lt)


def load(sems, *pairs):
    copies = [pltpu.make_async_copy(a, b, sems.at[i]) for i, (a, b) in enumerate(pairs)]
    for copy in copies:
        copy.start()
    for copy in copies:
        copy.wait()


def sums_body(inner_hbm, values_hbm, decays_hbm, sums, keep, send, sig, inner, values, decays, sems):
    copies = [pltpu.make_async_copy(decays_hbm, decays, sems.at[2 * TILES])]
    for lt in range(TILES):
        cols = slice(lt * LANES, (lt + 1) * LANES)
        for i, (source, target) in enumerate(((inner_hbm, inner), (values_hbm, values))):
            copies.append(pltpu.make_async_copy(source.at[:, cols], target.at[:, cols], sems.at[2 * lt + i]))
    for copy in copies:
        copy.start()
    copies[0].wait()
    for lt in range(TILES):
        cols = slice(lt * LANES, (lt + 1) * LANES)
        copies[1 + 2 * lt].wait()
        copies[2 + 2 * lt].wait()
        signal_tile(inner, values, sig, lt)
        fade = jnp.exp(-decays[:, cols])
        for group in range(0, MODES, 8):
            step = [jnp.broadcast_to(fade[r : r + 1], (BLOCKS, LANES)) for r in range(group, group + 8)]
            total = [sig[lt, pl.ds(0, BLOCKS, stride=SUB), :]] * 8
            for b in range(1, SUB):
                row = sig[lt, pl.ds(b, BLOCKS, stride=SUB), :]
                total = [t * e + row for t, e in zip(total, step)]
            for i in range(8):
                sums[lt, pl.ds(group + i, BLOCKS, stride=MODES), :] = total[i]
    core = lax.axis_index("core")
    for lt in range(TILES):
        cols = slice(lt * LANES, (lt + 1) * LANES)
        fade = jnp.exp(-decays[:, cols] * SUB)
        state = sums[lt, 0:MODES, :]
        for a in range(1, BLOCKS):
            state = state * fade + sums[lt, a * MODES : (a + 1) * MODES, :]
        place = slice((lt % 2) * LANES, (lt % 2 + 1) * LANES)

        @pl.when(core == lt // 2)
        def _():
            keep[:, place] = state

        @pl.when(core != lt // 2)
        def _():
            send[:, place] = state


def taps_body(inner_hbm, values_hbm, residues_hbm, decays_hbm, local, sig, inner, values, residues, decays, sems):
    load(sems, (inner_hbm, inner), (values_hbm, values), (residues_hbm, residues), (decays_hbm, decays))
    signal_into(inner, values, sig)
    for lt in range(TILES):
        cols = slice(lt * LANES, (lt + 1) * LANES)
        fade = jnp.exp(-decays[:, cols])
        weight = residues[:, cols]
        taps = []
        for lag in range(SUB):
            taps.append(jnp.broadcast_to(jnp.sum(weight, axis=0, keepdims=True), (BLOCKS, LANES)))
            weight = weight * fade
        rows = [sig[lt, pl.ds(b, BLOCKS, stride=SUB), :] for b in range(SUB)]
        for b in range(SUB):
            total = taps[0] * rows[b]
            for lag in range(1, b + 1):
                total = total + taps[lag] * rows[b - lag]
            local[lt, pl.ds(b, BLOCKS, stride=SUB), :] = total


def gate_body(outer, sums, local, near, far, residues, decays, gated, states, out):
    core = lax.axis_index("core")
    for lt in range(TILES):
        cols = slice(lt * LANES, (lt + 1) * LANES)
        place = slice((lt % 2) * LANES, (lt % 2 + 1) * LANES)
        fade = jnp.exp(-decays[:, cols] * SUB)
        weight = residues[:, cols]
        state = jnp.where(core == lt // 2, near[:, place], far[:, place])
        for a in range(BLOCKS):
            states[lt, a * MODES : (a + 1) * MODES, :] = state * weight
            if a + 1 < BLOCKS:
                state = state * fade + sums[lt, a * MODES : (a + 1) * MODES, :]
    for lt in range(TILES):
        cols = slice(lt * LANES, (lt + 1) * LANES)
        fade = jnp.exp(-decays[:, cols])
        step = [jnp.broadcast_to(fade[r : r + 1], (BLOCKS, LANES)) for r in range(MODES)]
        part = [states[lt, pl.ds(r, BLOCKS, stride=MODES), :] for r in range(MODES)]
        for b in range(SUB):
            part = [t * e for t, e in zip(part, step)]
            total = part
            while len(total) > 1:
                total = [total[i] + total[i + 1] for i in range(0, len(total), 2)]
            out[lt, pl.ds(b, BLOCKS, stride=SUB), :] = total[0] + local[lt, pl.ds(b, BLOCKS, stride=SUB), :]
    for lt in range(TILES):
        cols = slice(lt * LANES, (lt + 1) * LANES)
        result = (outer[:, cols].astype(F32) * out[lt]).astype(BF16)
        for copy in range(gated.shape[0]):
            gated[copy, :, cols] = result


def source_of(turn, shift):
    x, yhi = lax.axis_index("x"), lax.axis_index("yhi")
    z, ylo = lax.axis_index("z"), lax.axis_index("ylo")
    ahead = lax.rem(z + shift + 8 - 2 * (lax.rem(x, 2) * 2 + yhi), 8)
    odd = jnp.where((ahead >= 1) & (ahead <= 4), 1, 0)
    far = jnp.where(odd == 1, ahead - 1, lax.rem(8 - ahead, 8))
    turned = jnp.where(far == 0, 2, jnp.where(far == 1, 3, jnp.where(far == 2, 1, 0)))
    group = lax.rem(x + turned, 4) * 2 + lax.rem(ylo + turn + yhi, 2)
    return group, odd


def bundle_body(*refs):
    stacks, (out, sems) = refs[:-2], refs[-2:]
    copies, at = [], 0
    for i, stack in enumerate(stacks):
        count = stack.shape[0]
        copies.append(pltpu.make_async_copy(stack, out.at[at : at + count], sems.at[i]))
        at += count
    for copy in copies:
        copy.start()
    for copy in copies:
        copy.wait()


def bundle(stacks, cost=0):
    count = sum(stack.shape[0] for stack in stacks)
    return pl.pallas_call(
        bundle_body,
        out_shape=jax.ShapeDtypeStruct((count, 512, 256), BF16),
        in_specs=[pl.BlockSpec(memory_space=pl.ANY)] * len(stacks),
        out_specs=pl.BlockSpec(memory_space=pl.ANY),
        scratch_shapes=[pltpu.SemaphoreType.DMA((len(stacks),))],
        compiler_params=pltpu.CompilerParams(vmem_limit_bytes=VMEM_LIMIT),
        cost_estimate=pl.CostEstimate(flops=cost, bytes_accessed=count << 19, transcendentals=0),
    )(*stacks)


RANKS = [(dx, dy) for dx in (0, 3, 1, 2) for dy in range(2)]


def column_sums(places, stacks, gated, weight, sems):
    copies = []
    for stack in stacks:
        for i in range(stack.shape[0]):
            at = len(copies)
            group, odd = source_of(*places[at])
            copies.append(pltpu.make_async_copy(stack.at[i], weight.at[odd, group], sems.at[at]))
    for copy in copies:
        copy.start()
    for copy in copies:
        copy.wait()
    return [jnp.dot(gated[...], weight[odd].reshape(8 * 512, 256), preferred_element_type=F32) for odd in range(2)]


def own_body(places, count, *refs):
    pieces, stacks = refs[:8], refs[8 : 8 + count]
    total, gated, weight, row_sem, block_sem = refs[8 + count :]
    x, yhi = lax.axis_index("x"), lax.axis_index("yhi")
    copies = []
    for i, (piece, (dx, dy)) in enumerate(zip(pieces, RANKS)):
        rank = lax.rem(x + dx, 4) * 2 + lax.rem(yhi + dy, 2)
        columns = pl.ds(pl.multiple_of(rank * CHANS, CHANS), CHANS)
        copies.append(pltpu.make_async_copy(piece, gated.at[:, columns], row_sem.at[i]))
    for copy in copies:
        copy.start()
    for copy in copies:
        copy.wait()
    total[0], total[1] = column_sums(places, stacks, gated, weight, block_sem)


def other_body(places, count, *refs):
    total, gated, stacks = refs[0], refs[1], refs[2 : 2 + count]
    result, weight, block_sem = refs[2 + count :]
    core = lax.axis_index("core")
    for odd, theirs in enumerate(column_sums(places, stacks, gated, weight, block_sem)):
        mine, theirs = total[odd].astype(BF16), theirs.astype(BF16)
        result[:, odd * 512 : odd * 512 + 256] = jnp.where(core == 0, mine, theirs)
        result[:, odd * 512 + 256 : odd * 512 + 512] = jnp.where(core == 0, theirs, mine)


def project(places, pieces, own, other):
    blocks = [pltpu.VMEM((2, 8, 512, 256), BF16)]
    sems = [pltpu.SemaphoreType.DMA((16,))]
    params = pltpu.CompilerParams(vmem_limit_bytes=VMEM_LIMIT)
    cost = pl.CostEstimate(flops=1 << 35, bytes_accessed=6 << 20, transcendentals=0)
    total, gated = pl.pallas_call(
        lambda *refs: own_body(places, len(own), *refs),
        out_shape=[jax.ShapeDtypeStruct((2, ROWS, 256), F32), jax.ShapeDtypeStruct((ROWS, 8 * CHANS), BF16)],
        in_specs=[pl.BlockSpec(memory_space=pl.ANY)] * (8 + len(own)),
        out_specs=whole(2),
        scratch_shapes=blocks + [pltpu.SemaphoreType.DMA((8,))] + sems,
        compiler_params=params,
        cost_estimate=cost,
    )(*pieces, *own)
    return pl.pallas_call(
        lambda *refs: other_body(places, len(other), *refs),
        out_shape=jax.ShapeDtypeStruct((ROWS, 1024), BF16),
        in_specs=whole(2) + [pl.BlockSpec(memory_space=pl.ANY)] * len(other),
        out_specs=whole(1)[0],
        scratch_shapes=blocks + sems,
        compiler_params=params,
        cost_estimate=cost,
    )(total, gated, *other)


def ring(size, shift):
    return [(i, (i + shift) % size) for i in range(size)]


def swap(block):
    def number(x, yhi, ylo, z, core):
        return ((ylo * 8 + z) * 2 + core) * 8 + x * 2 + yhi

    pairs = []
    for x, yhi, ylo, z, core in np.ndindex(4, 2, 2, 8, 2):
        to_x, to_yhi = ylo * 2 + z // 4, z // 2 % 2
        far = (3, 2, 0, 1)[(x - to_x) % 4]
        to_z = (z + far if z % 2 else z - far) % 8
        pairs.append((number(x, yhi, ylo, z, core), number(to_x, to_yhi, yhi ^ to_yhi, to_z, core)))
    return lax.ppermute(block, ("ylo", "z", "core", "x", "yhi"), pairs)


def move(value, axis, shift):
    return lax.ppermute(value, axis, ring({"ylo": 2, "z": 8, "core": 2, "x": 4, "yhi": 2}[axis], shift))


def together(*values):
    return lax.optimization_barrier(values)


def shards(outer_gate, inner_gate, values, residues, decays, out_weight):
    first = swap(out_weight)
    tiled = jax.ShapeDtypeStruct((TILES, ROWS, LANES), F32)
    half = jax.ShapeDtypeStruct((MODES, HALF), F32)
    tile_scratch = pltpu.VMEM((TILES, ROWS, LANES), F32)
    work = ROWS * CHANS * MODES * 2
    shard, modes = pltpu.VMEM((ROWS, CHANS), BF16), pltpu.VMEM((MODES, CHANS), F32)
    full = pltpu.CompilerParams(vmem_limit_bytes=60 * 1024 * 1024)
    sums, keep, send = pl.pallas_call(
        sums_body,
        out_shape=[tiled, half, half],
        in_specs=[pl.BlockSpec(memory_space=pl.ANY)] * 3,
        out_specs=whole(3),
        scratch_shapes=[tile_scratch, shard, shard, modes, pltpu.SemaphoreType.DMA((2 * TILES + 1,))],
        compiler_params=full,
        cost_estimate=pl.CostEstimate(flops=work, bytes_accessed=2 << 20, transcendentals=0),
    )(inner_gate, values, decays)
    core, z, y = lax.axis_index("core"), lax.axis_index("z"), lax.axis_index("ylo")
    came = move(send, "core", 1)
    mine = lax.dynamic_slice_in_dim(decays, core * HALF, HALF, 1)
    fade = jnp.exp(-mine * ROWS)
    before = jnp.where(core == 0, keep, came)
    chip = fade * before + jnp.where(core == 0, came, keep)
    everyone = lax.all_to_all(jnp.broadcast_to(chip[None], (16, MODES, HALF)), ("ylo", "z"), 0, 0)
    first, late_inner = together(first, inner_gate)
    local = pl.pallas_call(
        taps_body,
        out_shape=tiled,
        in_specs=[pl.BlockSpec(memory_space=pl.ANY)] * 4,
        out_specs=whole(1)[0],
        scratch_shapes=[tile_scratch, shard, shard, modes, modes, pltpu.SemaphoreType.DMA((4,))],
        compiler_params=pltpu.CompilerParams(vmem_limit_bytes=VMEM_LIMIT),
        cost_estimate=pl.CostEstimate(flops=AHEAD, bytes_accessed=1 << 20, transcendentals=0),
    )(late_inner, values, residues, decays)
    chip_fade = fade * fade
    first = first[None]
    second, up_a, down_a = move(first, "ylo", 1), move(first, "z", 1), move(first, "z", -1)
    early, places = [first, second, up_a, down_a], [(0, 0), (1, 0), (0, 7), (0, 1)]
    place = y * 8 + z
    state = jnp.zeros_like(chip)
    for k in range(15):
        state = jnp.where(k < place, state * chip_fade + everyone[k], state)
    after = fade * state + before
    near = jnp.where(core == 0, state, after)
    far = move(jnp.where(core == 0, after, state), "core", 1)
    gated = call(
        gate_body, jax.ShapeDtypeStruct((1, ROWS, CHANS), BF16), [tile_scratch, tile_scratch], 0, 0,
        outer_gate, sums, local, near, far, residues, decays,
    )
    gated, second, up_a, down_a = together(gated, second, up_a, down_a)
    early = [first, second, up_a, down_a]
    near_b = [move(second, "z", 1), move(second, "z", -1)]
    up_a, down_a = move(up_a, "z", 1), move(down_a, "z", -1)
    early, places = early + [up_a, down_a], places + [(0, 6), (0, 2)]
    side = move(gated, "yhi", 1)
    side, *early = together(side, *early)
    early = bundle(early, 1 << 36)

    up_b, down_b = move(up_a, "ylo", 1), move(down_a, "ylo", 1)
    up_a, down_a = move(up_a, "z", 1), move(down_a, "z", -1)
    opposite = move(up_a, "z", 1)
    middle, places = [up_a, down_a, up_b, down_b, opposite], places + [(0, 5), (0, 3), (1, 6), (1, 2), (0, 4)]
    middle, places = middle + near_b, places + [(1, 7), (1, 1)]
    pair = jnp.concatenate([gated, side], axis=0)
    pair_up, pair_down = move(pair, "x", 1), move(pair, "x", -1)
    pair_up, pair_down, early, *middle = together(pair_up, pair_down, early, *middle)

    far_same, far_cross = move(pair_up[0], "x", 1), move(pair_down[1], "x", -1)
    late = [move(up_b, "z", 1), move(down_b, "z", -1), move(opposite, "ylo", 1)]
    places += [(1, 5), (1, 3), (1, 4)]
    far_same, far_cross, *late = together(far_same, far_cross, *late)
    pieces = [v[dy] for v in (pair, pair_up, pair_down) for dy in range(2)] + [far_same, far_cross]
    stacks = [early, bundle(middle, 1 << 36), bundle(late)]
    return project(places, pieces, stacks, [move(stack, "core", 1) for stack in stacks])


def solution(mesh):
    wide = Mesh(mesh.devices.reshape(2, 8, 2, 4, 2), ("ylo", "z", "core", "x", "yhi"))
    ctx, ch = ("ylo", "z", "core"), ("x", "yhi")
    return jax.shard_map(
        shards,
        mesh=wide,
        in_specs=(P(ctx, ch), P(ctx, ch), P(ctx, ch), P(None, ch), P(None, ch), P(ch, ctx)),
        out_specs=P(ctx, ch),
        check_vma=False,
    )
```
